32 devices in a mesh: snap: 2 (over x), blk: 16 (over z, y, core).
Axes of the slice: x: 2, y: 2, z: 4, core: 2. Of those that a mesh axis runs over, the one named last changes fastest.
Arguments:
- coeffs: bfloat16 [2, 3072, 12544], P(None, ('snap', 'blk')), parts along dimension 1, may hold values from -6 to 6
- k_plus_g: float32 [6, 12544], P('snap'), parts along dimension 0, may hold values from -2 to 2
- pairs: int32 [32, 2], P(('snap', 'blk')), parts along dimension 0, may hold values from 0 to 1, as said below
- levels: int32 [3072], P(('snap', 'blk')), parts along dimension 0, may hold values from 0 to 16
Outputs:
- velocity: float32 [3, 2, 3072, 480], P(None, None, ('snap', 'blk')), parts along dimension 2
The draws below stay inside these ranges and needn't reach their ends.
There are 2 independent parts, one for each index of `snap`. The reference program is written for one: setup_inputs(seed, part) draws one part's arguments, and reference() takes and returns one part's arrays. A program takes and returns all parts, laid end to end along the dimension named above; each array names one. Nothing has to cross between parts.
Inputs may be any that keep to these rules, and one draw needn't show every extreme that they name: In each row of pairs the ones come first; pairs[i, d-1] is 0 where i + d >= 16; row 0 holds 2 ones.
All inputs are finite; a program needn't handle non-finite values.
Results may differ from the reference program's by a relative error of at most 0.0029.
Values may be sent and summed in bfloat16 or wider, within the bound.
No kernel may reach another device: no remote copies, remote signals or barrier semaphores. Data moves between devices by JAX's collectives and lax.ppermute only.
A program may use at most 64 MiB of HBM per device.

```python
import math
import jax
import jax.numpy as jnp
from jax import lax

PW = 12544
REACH = 2
OCC_STEPS = 16
SPAN = 5
GROUPS = 16
BANDS = 1536


def draw_pairs(key, part):
    key = jax.random.fold_in(key, 7)
    reach = jax.random.randint(key, (GROUPS,), 0, REACH + 1)
    reach = reach.at[0].set(REACH)
    offsets = jnp.arange(1, REACH + 1, dtype=jnp.int32)
    rows = jnp.arange(GROUPS, dtype=jnp.int32)
    inside = (offsets[None, :] <= reach[:, None]) & (rows[:, None] + offsets[None, :] < GROUPS)
    return inside.astype(jnp.int32)


def set_ends(entries, key, least, high):
    longest = entries.shape.index(max(entries.shape))
    spots = []
    for shift in (0, 1):
        where = [jax.random.randint(jax.random.fold_in(key, axis), (), 0, length) for axis, length in enumerate(entries.shape)]
        where[longest] = (where[longest] + shift) % entries.shape[longest]
        spots.append(tuple(where))
    return entries.at[spots[0]].set(least).at[spots[1]].set(high)


def block_levels(own_key, dims, cuts, smallest, high):
    level, own = 1.0, jax.random.fold_in(own_key, 6)
    for axis_at, parts in cuts:
        heights = jnp.exp(jax.random.uniform(jax.random.fold_in(own, axis_at), (parts,), jnp.float32, smallest / len(cuts), high / len(cuts)))
        level = level * jnp.repeat(heights, dims[axis_at] // parts).reshape([-1 if axis == axis_at else 1 for axis in range(len(dims))])
    return level


def normal_values(stream_key, shape, deviation, bound, pieces=(), held_as=jnp.bfloat16):
    values = jax.random.normal(stream_key, shape, jnp.float32) * deviation
    if len(pieces) > 0:
        values = block_levels(stream_key, shape, pieces, -0.22, 0.18) * values
    return jnp.clip(values, min=-bound, max=bound).astype(held_as)


def setup_inputs(seed: int = 0, part: int = 0) -> dict:
    seeds = jax.random.split(jax.random.key(seed), 5)
    part_keys = jax.random.split(jax.random.fold_in(seeds[4], part), 5)
    coeffs = normal_values(part_keys[0], (2, BANDS, PW), 1.0, 6.0, ((1, 16),))
    k_plus_g = jnp.clip(jax.random.uniform(part_keys[1], (3, PW), jnp.float32, -2.0, 2.0), -2.0, 2.0)
    pairs = draw_pairs(jax.random.fold_in(jax.random.fold_in(seeds[4], part), 71), part)
    levels = set_ends(jax.random.randint(part_keys[3], (BANDS,), 0, OCC_STEPS + 1), jax.random.fold_in(part_keys[3], 1), 0, OCC_STEPS).astype(jnp.int32)
    return {"coeffs": coeffs, "k_plus_g": k_plus_g, "pairs": pairs, "levels": levels}


def tile_product(weighted, partner):
    prod = jnp.einsum('acnp,dmp->acdnm', weighted.astype(jnp.float32), partner.astype(jnp.float32))
    return jnp.stack([prod[:, 0, 0] + prod[:, 1, 1], prod[:, 0, 1] - prod[:, 1, 0]], axis=1)

def mirror(tile):
    return jnp.stack([-jnp.swapaxes(tile[..., 0, :, :], -1, -2), jnp.swapaxes(tile[..., 1, :, :], -1, -2)], axis=-3)

def reference(coeffs, k_plus_g, pairs, levels):
    groups = pairs.shape[0]
    bands = coeffs.shape[1] // groups
    plane = coeffs.shape[2]
    blocks = coeffs.reshape(2, groups, bands, plane)
    occup = (levels.astype(jnp.float32) / OCC_STEPS).reshape(groups, bands)
    live = pairs.astype(jnp.float32)
    scale = 1.0 / math.sqrt(plane)

    def upper_tiles(index):
        own = lax.dynamic_index_in_dim(blocks, index, 1, keepdims=False)
        weighted = (k_plus_g[:, None, None, :] * own[None].astype(jnp.float32)).astype(jnp.bfloat16)
        row = lax.dynamic_index_in_dim(live, index, 0, keepdims=False)
        occ_own = lax.dynamic_index_in_dim(occup, index, 0, keepdims=False)
        tiles = []
        for offset in range(REACH + 1):
            other = index + offset
            safe = jnp.minimum(other, groups - 1).astype(jnp.int32)
            partner = lax.dynamic_index_in_dim(blocks, safe, 1, keepdims=False)
            occ_part = lax.dynamic_index_in_dim(occup, safe, 0, keepdims=False)
            if offset == 0:
                flag = jnp.float32(1.0)
            else:
                flag = row[offset - 1] * (other < groups).astype(jnp.float32)
            weights = (occ_own[:, None] - occ_part[None, :]) * (flag * scale)
            tiles.append(tile_product(weighted, partner) * weights)
        return jnp.stack(tiles, axis=0)
    upper = lax.map(upper_tiles, jnp.arange(groups, dtype=jnp.int32))
    slots = []
    for offset in range(-REACH, REACH + 1):
        if offset >= 0:
            slots.append(upper[:, offset])
        else:
            down = -offset
            flipped = mirror(upper[:, down])
            slots.append(jnp.concatenate([jnp.zeros_like(flipped[:down]), flipped[:groups - down]], axis=0))
    stacked = jnp.stack(slots, axis=4)
    return jnp.transpose(stacked, (1, 2, 0, 3, 4, 5)).reshape(3, 2, groups * bands, SPAN * bands)
```

```python
import functools
import math

import jax
import jax.numpy as jnp
from jax import lax
from jax.experimental import pallas as pl
from jax.experimental.pallas import tpu as pltpu
from jax.sharding import PartitionSpec as P

REACH = 2
OCC_STEPS = 16
SPAN = 5
LANES = 128
SECOND = (28, 14, 7)
PIECE = 7
F32 = jnp.float32
BF16 = jnp.bfloat16
VMEM_BYTES = 62 * 2**20


def product(k, low, high):
    wide = low.astype(F32)
    rows = jnp.concatenate([(k[a][None, :] * wide[c]).astype(BF16) for c in range(2) for a in range(3)], axis=0)
    cols = jnp.concatenate([high[0], high[1]], axis=0)
    return lax.dot_general(rows, cols, (((1,), (1,)), ((), ())), preferred_element_type=F32)


def combine(acc):
    rows, bands = acc.shape[0] // 2, acc.shape[1] // 2
    up, down = acc[:rows], acc[rows:]
    return jnp.concatenate([up[:, :bands] + down[:, bands:], up[:, bands:] - down[:, :bands]], axis=1)


def weights_of(low, high, offset, scale):
    bands = low.shape[1]
    low, high = low.astype(F32), high.astype(F32)
    flag = low[1, 0:1, bands + offset - 1 : bands + offset] if offset else 1.0
    weights = (low[0][:, :bands] - high[1][:, :bands]) * (flag * scale)
    weights = jnp.concatenate([weights] * 3, axis=0)
    return jnp.concatenate([weights, weights], axis=1)


def pack(tile):
    rows = tile.shape[0]
    rest = tile[:, LANES:]
    return jnp.concatenate([tile[:, :LANES], jnp.concatenate([rest[: rows // 2], rest[rows // 2 :]], axis=1)], axis=0)


def unpack(packed):
    rows = packed.shape[0] * 2 // 3
    rest = packed[rows:]
    width = LANES // 2
    return jnp.concatenate([packed[:rows], jnp.concatenate([rest[:, :width], rest[:, width:]], axis=0)], axis=1)


def roles(kind, info):
    early, side, core = info[0], info[1], info[2]
    if kind == "diag":
        return 1, 0, (0,)
    if kind == "near":
        return 1, core, (1 - core,)
    if kind == "early":
        return early, side, (1 - side, 1 - side, side)
    return 1 - early, side, (1 - side, side, side)


OFFSETS = {"diag": (0,), "near": (1,), "early": (2, 1, 2), "late": (2, 1, 2)}


def pair_body(kind, has_start, steps, step, begin, ends, scale, info, k_ref, x_ref, *refs):
    offsets = OFFSETS[kind]
    count = len(offsets)
    active, half, others = roles(kind, info)
    q_refs, refs = refs[:count], refs[count:]
    if ends:
        facts_x, facts_q, refs = refs[0], refs[1 : 1 + count], refs[1 + count :]
    if has_start:
        start, refs = refs[0], refs[1:]
    outs, acc = refs[:-1], refs[-1]
    at = pl.program_id(0)

    def each(run):
        for i in range(count):
            if offsets[i] == 0:
                run(i, x_ref, x_ref, *([facts_x] * 2 if ends else [None] * 2))
                continue
            facts = (facts_q[i], facts_x) if ends else (None, None)
            pl.when(others[i] == 1)(lambda: run(i, q_refs[i], x_ref, facts[0], facts[1]))
            pl.when(others[i] == 0)(lambda: run(i, x_ref, q_refs[i], facts[1], facts[0]))

    @pl.when(active == 1)
    def _():
        first = half * (k_ref.shape[1] // 2 // LANES) + begin + at * step
        k = k_ref[:, pl.ds(pl.multiple_of(first * LANES, LANES), step * LANES)]

        def add(i, low, high, facts_low, facts_high):
            part = product(k, low[...], high[...])

            @pl.when(at == 0)
            def _():
                acc[i] = part

            @pl.when(at > 0)
            def _():
                acc[i] += part

        each(add)

        @pl.when(at == steps - 1)
        def _():
            if not ends:
                for i in range(count):
                    tile = combine(acc[i])
                    outs[0][i] = tile + start[i] if has_start else tile
                return

            def end(i, low, high, facts_low, facts_high):
                tile = combine(acc[i])
                if has_start:
                    tile = tile + start[i]
                tile = tile * weights_of(facts_low[...], facts_high[...], offsets[i], scale)
                if i == 0:
                    outs[0][...] = tile
                if len(outs) > 1:
                    outs[1][i] = pack(tile).astype(BF16)

            each(end)

    if not isinstance(active, int):
        @pl.when((active == 0) & (at == 0))
        def _():
            for out in outs:
                out[...] = jnp.zeros_like(out)


def pair_sums(kind, info, k, x, partners, begin, start, steps, step, facts):
    width = step * LANES
    bands = x[0].shape[1]
    count = len(partners)
    ends = facts is not None
    shape = (count, 3 * bands, 2 * bands)

    def block(at):
        return pl.BlockSpec((2, bands, width), lambda j, info: (0, 0, at + j * roles(kind, info)[0]))

    whole = lambda shape: pl.BlockSpec(shape, lambda j, info: (0,) * len(shape))
    in_specs = [whole(k.shape), block(x[1])] + [block(at) for _, at in partners]
    operands = [k, x[0]] + [q for q, _ in partners]
    if ends:
        in_specs += [pl.BlockSpec((2, bands, LANES), lambda j, info, at=at: (0, 0, at)) for _, at in facts]
        operands += [array for array, _ in facts]
    if start is not None:
        in_specs.append(whole(shape))
        operands.append(start)
    if ends:
        out_shape = [jax.ShapeDtypeStruct(shape[1:], F32)]
        if kind != "diag":
            out_shape.append(jax.ShapeDtypeStruct((count, 9 * bands // 2, LANES), BF16))
    else:
        out_shape = [jax.ShapeDtypeStruct(shape, F32)]
    return pl.pallas_call(
        functools.partial(pair_body, kind, start is not None, steps, step, begin, ends, 1.0 / math.sqrt(k.shape[1])),
        grid_spec=pltpu.PrefetchScalarGridSpec(
            num_scalar_prefetch=1,
            grid=(steps,),
            in_specs=in_specs,
            out_specs=[whole(s.shape) for s in out_shape],
            scratch_shapes=[pltpu.VMEM((count, 6 * bands, 2 * bands), F32)],
        ),
        out_shape=out_shape,
        compiler_params=pltpu.CompilerParams(vmem_limit_bytes=VMEM_BYTES),
        cost_estimate=pl.CostEstimate(flops=1000, bytes_accessed=1000, transcendentals=0),
        name=kind,
    )(info, *operands)


def halves_body(which, cuts, with_facts, info, levels, pairs, coeffs, *refs):
    outs, held, sems = refs[: len(cuts)], refs[-2], refs[-1]
    bands = coeffs.shape[1]
    half = coeffs.shape[2] // 2
    count = half // (PIECE * LANES)
    base = half * (info[2] if which == 0 else 1 - info[2])
    span = lambda start, size: pl.ds(start * LANES, size * LANES)
    loads = []
    for i in range(count):
        source = pl.ds(pl.multiple_of(base + i * PIECE * LANES, LANES), PIECE * LANES)
        loads.append(pltpu.make_async_copy(coeffs.at[:, :, source], held.at[:, :, span(i * PIECE, PIECE)], sems.at[0, i]))
        loads[-1].start()
    occup = levels[...].astype(F32) / OCC_STEPS
    spread = jnp.broadcast_to(occup, (bands, bands))
    lane = lax.broadcasted_iota(jnp.int32, (bands, LANES - bands), 1)
    flags = jnp.zeros((bands, LANES - bands), F32)
    for d in range(REACH):
        flags = jnp.where(lane == d, pairs[0, d].astype(F32), flags)
    last = span(count * PIECE, 1)
    held[0, :, last] = jnp.concatenate([spread.T, jnp.zeros_like(flags)], axis=1).astype(BF16)
    held[1, :, last] = jnp.concatenate([spread, flags], axis=1).astype(BF16)
    stores = []

    def store(out, i, start, at, size):
        copy = pltpu.make_async_copy(held.at[:, :, span(start, size)], outs[out].at[:, :, span(at, size)], sems.at[1 + out, i])
        copy.start()
        stores.append(copy)

    for out, (start, size) in enumerate(cuts):
        if with_facts[out]:
            store(out, count, count * PIECE, size, 1)
    for i in range(count):
        loads[i].wait()
        for out, (start, size) in enumerate(cuts):
            if start <= i * PIECE < start + size:
                store(out, i, i * PIECE, i * PIECE - start, PIECE)
    for copy in stores:
        copy.wait()


def halves(which, cuts, with_facts, info, levels, pairs, coeffs, name):
    bands = coeffs.shape[1]
    anywhere = pl.BlockSpec(memory_space=pl.ANY)
    return pl.pallas_call(
        functools.partial(halves_body, which, cuts, with_facts),
        in_specs=[
            pl.BlockSpec(memory_space=pltpu.SMEM),
            pl.BlockSpec(memory_space=pltpu.VMEM),
            pl.BlockSpec(memory_space=pltpu.SMEM),
            anywhere,
        ],
        out_specs=[anywhere] * len(cuts),
        out_shape=[
            jax.ShapeDtypeStruct((2, bands, (size + int(more)) * LANES), BF16) for (_, size), more in zip(cuts, with_facts)
        ],
        scratch_shapes=[
            pltpu.VMEM((2, bands, coeffs.shape[2] // 2 + LANES), BF16),
            pltpu.SemaphoreType.DMA((1 + len(cuts), coeffs.shape[2] // 2 // LANES // PIECE + 1)),
        ],
        compiler_params=pltpu.CompilerParams(vmem_limit_bytes=VMEM_BYTES),
        cost_estimate=pl.CostEstimate(flops=1000, bytes_accessed=1000, transcendentals=0),
        name=name,
    )(info, levels[None, :], pairs, coeffs)


def final_body(info, diag, own, core, early, late, side, up_y, down_y, up_z, down_z, cross, out):
    bands = out.shape[2]
    first = info[0] == 1
    low = info[1] == 0
    wide = lambda ref: unpack(ref[...].astype(F32))
    received = [unpack(up_y[i].astype(F32) + down_y[i].astype(F32)) for i in range(3)]
    far = unpack(up_z[...].astype(F32) + down_z[...].astype(F32))
    mine = own[...] + unpack(core[0].astype(F32))
    near1 = jnp.where(first, mine, received[1] + unpack(side[1].astype(F32)))
    near2 = early[...] + late[...] + received[0]
    away1 = jnp.where(first, received[1] + wide(cross), mine)
    away2 = received[2] + far
    above = [jnp.where(low, near1, away1), jnp.where(low, near2, away2)]
    below = [jnp.where(low, away1, near1), jnp.where(low, away2, near2)]
    for a in range(3):
        for part in range(2):
            cut = lambda tile: tile[a * bands : (a + 1) * bands, part * bands : (part + 1) * bands]
            turn = lambda tile: -cut(tile).T if part == 0 else cut(tile).T
            out[a, part] = jnp.concatenate([turn(below[1]), turn(below[0]), cut(diag), cut(above[0]), cut(above[1])], axis=1)


def final(info, bands, *operands):
    vmem = pl.BlockSpec(memory_space=pltpu.VMEM)
    return pl.pallas_call(
        final_body,
        in_specs=[pl.BlockSpec(memory_space=pltpu.SMEM)] + [vmem] * len(operands),
        out_specs=vmem,
        out_shape=jax.ShapeDtypeStruct((3, 2, bands, SPAN * bands), F32),
        compiler_params=pltpu.CompilerParams(vmem_limit_bytes=VMEM_BYTES),
        name="final",
    )(info, *operands)


def routes(groups):
    quads = range(groups // 4)
    at = lambda q, side, core: 4 * q + 2 * side + core
    early = lambda q, side: at(q, side, side)
    late = lambda q, side: at(q, side, 1 - side)
    away = lambda q, side: q + 1 - 2 * side
    both = [(q, side) for q in quads for side in (0, 1)]
    other = [(at(q, s, c), at(q, s, 1 - c)) for q, s in both for c in (0, 1)]
    y_early = [(late(q, 1 - s), early(q, s)) for q, s in both]
    y_late = [(early(q, 1 - s), late(q, s)) for q, s in both]
    ok = [(q, s) for q, s in both if 0 <= away(q, s) < groups // 4]
    z_early = [(early(away(q, s), s), early(q, s)) for q, s in ok]
    z_late = [(late(away(q, s), s), late(q, s)) for q, s in ok]
    forward = [(early(q, s), late(q, s)) for q, s in both]
    turn = lambda route: [(b, a) for a, b in route]
    cross = [(late(q, s), early(away(q, s), s)) for q, s in ok]
    return dict(
        other=other, y_early=y_early, y_late=y_late, z_early=z_early, z_late=z_late, forward=forward,
        tile_y_early=turn(y_early), tile_y_late=turn(y_late), tile_z_early=turn(z_early), tile_z_late=turn(z_late), cross=cross,
    )


def after(value, *first):
    return lax.optimization_barrier((value, *first))[0]


def shards(coeffs, k_plus_g, pairs, levels):
    groups = lax.axis_size("blk")
    me = lax.axis_index("blk")
    bands, plane = coeffs.shape[1:]
    tiles = plane // 2 // LANES
    core = me % 2
    side = (me // 2) % 2
    info = jnp.stack([(core == side).astype(jnp.int32), side, core])
    way = routes(groups)
    send = lambda value, name: lax.ppermute(value, "blk", way[name])

    (first,) = halves(0, [(0, tiles)], [True], info, levels, pairs, coeffs, "first")
    y_first, z_first = send(first, "y_early"), send(first, "z_early")
    begins = [sum(SECOND[:i]) for i in range(len(SECOND))]
    swap, *second = halves(
        1, [(0, tiles)] + list(zip(begins, SECOND)), [True, True] + [False] * (len(SECOND) - 1), info, levels, pairs,
        after(coeffs, first), "second",
    )
    swapped = send(swap, "other")

    here, facts_y, facts_core, facts_z = (first, tiles), (y_first, tiles), (swapped, tiles), (z_first, tiles)
    (diag,) = pair_sums("diag", info, k_plus_g, (after(coeffs, swap), 0), [(coeffs, 0)], 0, None, 7, 14, [here, here])
    own, own_packed = pair_sums(
        "near", info, k_plus_g, (swapped, 0), [(after(first, diag), 0)], 0, None, 7, 7, [facts_core, here]
    )
    tile_core = send(own_packed, "other")

    y_second, z_second = [], []

    def send_second(block, *first):
        block = after(block, *first)
        y_second.append(send(block, "y_late"))
        z_second.append(send(block, "z_late"))

    send_second(second[0], own)
    forward = send(after(z_first, own), "forward")
    send_second(second[1], own, y_first, z_first)
    early_tile, early_tiles = pair_sums(
        "early", info, k_plus_g, (y_first, 0), [(after(first, own), 0), (swapped, 0), (z_first, 0)], 0, None, 7, 7,
        [facts_y, here, facts_core, facts_z],
    )
    tile_y_early = send(early_tiles, "tile_y_early")
    tile_side = send(early_tiles, "forward")
    tile_z_early = send(early_tiles[2], "tile_z_early")
    send_second(second[2], early_tiles, y_second[0], z_second[0])

    sums = None
    for i, (begin, size) in enumerate(zip(begins, SECOND)):
        step = 14 if size % 14 == 0 else 7
        ends = i == len(SECOND) - 1
        out = pair_sums(
            "late", info, k_plus_g, (y_second[i], 0), [(after(second[i], early_tiles), 0), (forward, begin // step), (z_second[i], 0)],
            begin, sums, size // step, step,
            [(y_second[0], SECOND[0]), here, (forward, tiles), (z_second[0], SECOND[0])] if ends else None,
        )
        sums = out[0]
    late_tile, late_tiles = out
    tile_y_late = send(late_tiles, "tile_y_late")
    tile_z_late = send(late_tiles[2], "tile_z_late")
    cross = send(late_tiles[1], "cross")
    return final(
        info, bands, diag, own, tile_core, early_tile, late_tile, tile_side, tile_y_early, tile_y_late, tile_z_early, tile_z_late, cross
    )


def solution(mesh):
    in_specs = (
        P(None, ("snap", "blk"), None),
        P("snap", None),
        P(("snap", "blk"), None),
        P(("snap", "blk")),
    )
    out_specs = P(None, None, ("snap", "blk"), None)
    return jax.shard_map(shards, mesh=mesh, in_specs=in_specs, out_specs=out_specs, check_vma=False)
```

```python
import functools
import math

import jax
import jax.numpy as jnp
from jax import lax
from jax.experimental import pallas as pl
from jax.experimental.pallas import tpu as pltpu
from jax.sharding import PartitionSpec as P

REACH = 2
OCC_STEPS = 16
SPAN = 5
LANES = 128
CHUNKS = (24, 25)
F32 = jnp.float32
BF16 = jnp.bfloat16
VMEM_BYTES = 62 * 2**20


def product(k, low, high):
    dims = (((1,), (1,)), ((), ()))
    wide = low.astype(F32)
    rows = [jnp.concatenate([(k[a][None, :] * wide[c]).astype(BF16) for a in range(3)], axis=0) for c in range(2)]
    straight = jnp.concatenate([high[0], high[1]], axis=0)
    turned = jnp.concatenate([high[1], -high[0]], axis=0)
    first = lax.dot_general(rows[0], straight, dims, preferred_element_type=F32)
    return first + lax.dot_general(rows[1], turned, dims, preferred_element_type=F32)


def weights_of(low, high, offset, scale):
    bands = low.shape[1]
    low, high = low.astype(F32), high.astype(F32)
    if isinstance(offset, int):
        flag = low[1, 0:1, bands + offset - 1 : bands + offset] if offset else 1.0
    else:
        flag = jnp.where(offset == 1, low[1, 0:1, bands : bands + 1], low[1, 0:1, bands + 1 : bands + 2])
    weights = (low[0][:, :bands] - high[1][:, :bands]) * (flag * scale)
    weights = jnp.concatenate([weights] * 3, axis=0)
    return jnp.concatenate([weights, weights], axis=1)


def pack(tile):
    rows = tile.shape[0]
    rest = tile[:, LANES:]
    return jnp.concatenate([tile[:, :LANES], jnp.concatenate([rest[: rows // 2], rest[rows // 2 :]], axis=1)], axis=0)


def unpack(packed):
    rows = packed.shape[0] * 2 // 3
    rest = packed[rows:]
    width = LANES // 2
    return jnp.concatenate([packed[:rows], jnp.concatenate([rest[:, :width], rest[:, width:]], axis=0)], axis=1)


OFFSETS = {"diag": (0,), "near": (1,), "far": (2, 1, 2)}


def roles(kind, info):
    first, side, core = info[0], info[1], info[2]
    if kind == "diag":
        return 0, (0,)
    if kind == "near":
        return core, (1 - core,)
    return side, (1 - side, jnp.where(first == 1, 1 - side, side), side)


def pick(values, i):
    out = values[0]
    for j in range(1, len(values)):
        out = jnp.where(i == j, values[j], out)
    return out


def pair_body(kind, first_tile, tiles, plans, facts_plans, has_start, scale, info, k_hbm, *refs):
    offsets = OFFSETS[kind]
    count, blocks = len(offsets), len(plans)
    half, others = roles(kind, info)
    ends = facts_plans is not None
    refs = list(refs)
    take = lambda number: [refs.pop(0) for _ in range(number)]
    sources = [take(len(plan)) for plan in plans]
    facts_sources = [take(len(plan)) for plan in facts_plans] if ends else []
    start_hbm = take(1)[0] if has_start else None
    outs = take(len(refs) - 9)
    k_held, held, facts, start, acc, sems, k_sem, facts_sems, start_sem = refs

    half_tiles = k_hbm.shape[1] // 2 // LANES
    first = half * half_tiles + first_tile
    k_copy = pltpu.make_async_copy(k_hbm.at[:, pl.ds(pl.multiple_of(first * LANES, LANES), tiles * LANES)], k_held, k_sem)

    def copies(plan, arrays, into, size, sems):
        out = []
        for n, (array, (where, at)) in enumerate(zip(arrays, plan)):
            when = None if where is None else info[0] == 1 if "first" in where else info[0] == 0 if "second" in where else None
            at += 0 if where is None else info[1] * half_tiles if "side" in where else info[2] * half_tiles if "core" in where else 0
            span = pl.ds(at * LANES if isinstance(at, int) else pl.multiple_of(at * LANES, LANES), size * LANES)
            out.append((when, pltpu.make_async_copy(array.at[:, :, span], into, sems.at[n])))
        return out

    def each(copies, run):
        for when, copy in copies:
            if when is None:
                run(copy)
            else:
                pl.when(when)(functools.partial(run, copy))

    begin = lambda copies: each(copies, lambda copy: copy.start())
    wait = lambda copies: each(copies, lambda copy: copy.wait())
    loads = [copies(plans[b], sources[b], held.at[b], tiles, sems.at[b]) for b in range(blocks)]
    later = []
    if ends:
        for b in range(blocks):
            later += copies(facts_plans[b], facts_sources[b], facts.at[b], 1, facts_sems.at[b])
    if has_start:
        later.append((None, pltpu.make_async_copy(start_hbm, start, start_sem)))
    k_copy.start()
    for load in loads[:2]:
        begin(load)
    begin(later)
    k_copy.wait()
    wait(loads[0])

    def order(i):
        if kind == "diag":
            return 0, 0
        other = pick(others, i) == 1
        return jnp.where(other, i + 1, 0), jnp.where(other, 0, i + 1)

    @pl.loop(0, count)
    def _(i):
        for j in range(1, blocks):
            @pl.when(i == j - 1)
            def _():
                wait(loads[j])
                if j == 1:
                    for load in loads[2:]:
                        begin(load)

        low, high = order(i)
        acc[i] = product(k_held[...], held[low], held[high])

    wait(later)

    @pl.loop(0, count)
    def _(i):
        tile = acc[i]
        if has_start:
            tile = tile + start[i]
        if not ends:
            outs[0][i] = tile
            return
        low, high = order(i)
        tile = tile * weights_of(facts[low], facts[high], 0 if kind == "diag" else pick(offsets, i), scale)

        @pl.when(i == 0)
        def _():
            outs[0][...] = tile

        if len(outs) > 1:
            packed = pack(tile).astype(BF16)
            outs[1][i] = packed
        for j in range(2, len(outs)):
            @pl.when(i == j - 1)
            def _():
                outs[j][...] = packed


def pair_sums(kind, info, k, blocks, begin, tiles, facts=None, start=None):
    bands = blocks[0][0][0].shape[1]
    count = len(OFFSETS[kind])
    ends = facts is not None
    shape = (count, 3 * bands, 2 * bands)
    arrays = lambda blocks: [part[0] for block in blocks for part in block]
    plans = lambda blocks: tuple(tuple((part[1], part[2]) for part in block) for block in blocks)
    operands = [k] + arrays(blocks) + arrays(facts or []) + ([] if start is None else [start])
    packed = (9 * bands // 2, LANES)
    if not ends:
        out_shape = [jax.ShapeDtypeStruct(shape, F32)]
    else:
        out_shape = [jax.ShapeDtypeStruct(shape[1:], F32)]
        if kind != "diag":
            out_shape.append(jax.ShapeDtypeStruct((count, *packed), BF16))
        if count == 3:
            out_shape += [jax.ShapeDtypeStruct(packed, BF16)] * 2
    return pl.pallas_call(
        functools.partial(
            pair_body, kind, begin, tiles, plans(blocks), plans(facts) if ends else None, start is not None, 1.0 / math.sqrt(k.shape[1])
        ),
        in_specs=[pl.BlockSpec(memory_space=pltpu.SMEM)] + [pl.BlockSpec(memory_space=pl.ANY)] * len(operands),
        out_specs=[pl.BlockSpec(memory_space=pltpu.VMEM)] * len(out_shape),
        out_shape=out_shape,
        scratch_shapes=[
            pltpu.VMEM((k.shape[0], tiles * LANES), F32),
            pltpu.VMEM((len(blocks), 2, bands, tiles * LANES), BF16),
            pltpu.VMEM((len(blocks), 2, bands, LANES), BF16),
            pltpu.VMEM(shape, F32),
            pltpu.VMEM(shape, F32),
            pltpu.SemaphoreType.DMA((len(blocks), 2)),
            pltpu.SemaphoreType.DMA,
            pltpu.SemaphoreType.DMA((len(blocks), 2)),
            pltpu.SemaphoreType.DMA,
        ],
        compiler_params=pltpu.CompilerParams(vmem_limit_bytes=VMEM_BYTES),
        cost_estimate=pl.CostEstimate(flops=1000, bytes_accessed=1000, transcendentals=0),
        name=kind,
    )(info, *operands)


def pieces_body(cuts, info, levels, pairs, coeffs, *refs):
    outs, held, sems = refs[: len(cuts)], refs[-2], refs[-1]
    bands = coeffs.shape[1]
    half = coeffs.shape[2] // 2
    tiles = half // LANES
    side, core = info[1], info[2]
    span = lambda start, size: pl.ds(pl.multiple_of(start, LANES), size * LANES)
    loads, stores, at = [], [], 1
    for n, (which, start, size, more) in enumerate(cuts):
        source = half * {"y": 1 - side, "z": side, "core": 1 - core}[which] + start * LANES
        if size == 0:
            continue
        here = held.at[:, :, span(at * LANES, size)]
        loads.append(pltpu.make_async_copy(coeffs.at[:, :, span(source, size)], here, sems.at[0, n]))
        loads[-1].start()
        stores.append(pltpu.make_async_copy(here, outs[n].at[:, :, span(0, size)], sems.at[1, n]))
        at += size
    if any(more for *_, more in cuts):
        occup = levels[...].astype(F32) / OCC_STEPS
        spread = jnp.broadcast_to(occup, (bands, bands))
        lane = lax.broadcasted_iota(jnp.int32, (bands, LANES - bands), 1)
        flags = jnp.zeros((bands, LANES - bands), F32)
        for d in range(REACH):
            flags = jnp.where(lane == d, pairs[0, d].astype(F32), flags)
        held[0, :, :LANES] = jnp.concatenate([spread.T, jnp.zeros_like(flags)], axis=1).astype(BF16)
        held[1, :, :LANES] = jnp.concatenate([spread, flags], axis=1).astype(BF16)
    facts = []
    for n, (_, _, size, more) in enumerate(cuts):
        if more:
            facts.append(pltpu.make_async_copy(held.at[:, :, span(0, 1)], outs[n].at[:, :, span(size * LANES, 1)], sems.at[2, n]))
            facts[-1].start()
    for load, store in zip(loads, stores):
        load.wait()
        store.start()
    for copy in stores + facts:
        copy.wait()


def pieces(cuts, info, levels, pairs, coeffs, name):
    bands = coeffs.shape[1]
    anywhere = pl.BlockSpec(memory_space=pl.ANY)
    return list(
        pl.pallas_call(
            functools.partial(pieces_body, cuts),
            in_specs=[
                pl.BlockSpec(memory_space=pltpu.SMEM),
                pl.BlockSpec(memory_space=pltpu.VMEM),
                pl.BlockSpec(memory_space=pltpu.SMEM),
                anywhere,
            ],
            out_specs=[anywhere] * len(cuts),
            out_shape=[jax.ShapeDtypeStruct((2, bands, (size + int(more)) * LANES), BF16) for _, _, size, more in cuts],
            scratch_shapes=[
                pltpu.VMEM((2, bands, (1 + sum(size for _, _, size, _ in cuts)) * LANES), BF16),
                pltpu.SemaphoreType.DMA((3, len(cuts))),
            ],
            compiler_params=pltpu.CompilerParams(vmem_limit_bytes=VMEM_BYTES),
            cost_estimate=pl.CostEstimate(flops=1000, bytes_accessed=1000, transcendentals=0),
            name=name,
        )(info, levels[None, :], pairs, coeffs)
    )


def final_body(info, diag, own, core, far, up_y, up_z, ring, out):
    bands = out.shape[2]
    first = info[0] == 1
    low = info[1] == 0
    wide = lambda tile: unpack(tile.astype(F32))
    received = [wide(up_y[i]) for i in range(3)]
    mine = own[...] + wide(core[0])
    near1 = jnp.where(first, mine, received[1] + wide(ring[...]))
    near2 = far[...] + received[0]
    away1 = jnp.where(first, received[1] + wide(ring[...]), mine)
    away2 = received[2] + wide(up_z[...])
    above = [jnp.where(low, near1, away1), jnp.where(low, near2, away2)]
    below = [jnp.where(low, away1, near1), jnp.where(low, away2, near2)]
    for a in range(3):
        for part in range(2):
            cut = lambda tile: tile[a * bands : (a + 1) * bands, part * bands : (part + 1) * bands]
            turn = lambda tile: -cut(tile).T if part == 0 else cut(tile).T
            out[a, part] = jnp.concatenate([turn(below[1]), turn(below[0]), cut(diag), cut(above[0]), cut(above[1])], axis=1)


def final(info, bands, *operands):
    vmem = pl.BlockSpec(memory_space=pltpu.VMEM)
    return pl.pallas_call(
        final_body,
        in_specs=[pl.BlockSpec(memory_space=pltpu.SMEM)] + [vmem] * len(operands),
        out_specs=vmem,
        out_shape=jax.ShapeDtypeStruct((3, 2, bands, SPAN * bands), F32),
        compiler_params=pltpu.CompilerParams(vmem_limit_bytes=VMEM_BYTES),
        name="final",
    )(info, *operands)


def routes(groups):
    at = lambda q, side, core: 4 * q + 2 * side + core
    first = lambda q, side: at(q, side, side)
    second = lambda q, side: at(q, side, 1 - side)
    away = lambda q, side: q + 1 - 2 * side
    both = [(q, side) for q in range(groups // 4) for side in (0, 1)]
    ok = [(q, s) for q, s in both if 0 <= away(q, s) < groups // 4]
    z = [(at(away(q, s), s, c), at(q, s, c)) for q, s in ok for c in (0, 1)]
    return dict(
        core=[(at(q, s, c), at(q, s, 1 - c)) for q, s in both for c in (0, 1)],
        y=[(at(q, s, c), at(q, 1 - s, c)) for q, s in both for c in (0, 1)],
        z=z,
        back=[(b, a) for a, b in z],
        forward=[(first(q, s), second(q, s)) for q, s in both],
        ring=[(first(q, s), second(q, s)) for q, s in both] + [(second(q, s), first(away(q, s), s)) for q, s in ok],
    )


def shards(coeffs, k_plus_g, pairs, levels):
    groups = lax.axis_size("blk")
    me = lax.axis_index("blk")
    bands, plane = coeffs.shape[1:]
    tiles = plane // 2 // LANES
    core = me % 2
    side = (me // 2) % 2
    info = jnp.stack([(core == side).astype(jnp.int32), side, core])
    way = routes(groups)
    send = lambda value, name: lax.ppermute(value, "blk", way[name])
    tie = lambda *arrays: lax.optimization_barrier(arrays)

    one, two = CHUNKS
    swapped = send(coeffs, "core")
    y_one, z_one, facts = pieces(
        [("y", 0, one, False), ("z", 0, one, False), ("y", 0, 0, True)], info, levels, pairs, coeffs, "one"
    )
    facts_core = [(send(facts, "core"), None, 0)]
    coeffs, y_one, z_one = tie(coeffs, y_one, z_one)
    got_z, got_y = [send(z_one, "z")], [send(y_one, "y")]
    y_two, z_two = pieces([("y", one, two, True), ("z", one, two, True)], info, levels, pairs, coeffs, "two")
    got_z.append(send(z_two, "z"))
    got_y.append(send(y_two, "y"))
    here = [(facts, None, 0)]

    coeffs, y_two, z_two = tie(coeffs, y_two, z_two)
    (diag,) = pair_sums("diag", info, k_plus_g, [[(coeffs, None, 0)]], 0, 2 * tiles, [here])
    diag, swapped, coeffs = tie(diag, swapped, coeffs)
    own, own_packed = pair_sums(
        "near", info, k_plus_g, [[(swapped, "core", 0)], [(coeffs, "core", 0)]], 0, tiles, [facts_core, here]
    )
    tile_own = send(own_packed, "core")
    got_y[0], got_z[0], own = tie(got_y[0], got_z[0], own)
    forward = [send(got_z[0], "forward")]
    (sums,) = pair_sums(
        "far", info, k_plus_g,
        [[(got_y[0], None, 0)], [(coeffs, "side", 0)], [(swapped, "first side", 0), (forward[0], "second", 0)], [(got_z[0], None, 0)]], 0, one,
    )
    got_y[1], got_z[1], sums = tie(got_y[1], got_z[1], sums)
    forward.append(send(got_z[1], "forward"))
    far, far_packed, far_1, far_2 = pair_sums(
        "far", info, k_plus_g,
        [[(got_y[1], None, 0)], [(coeffs, "side", one)], [(swapped, "first side", one), (forward[1], "second", 0)], [(got_z[1], None, 0)]],
        one, two,
        [[(got_y[1], None, two)], here, [(facts_core[0][0], "first", 0), (forward[1], "second", two)], [(got_z[1], None, two)]], sums,
    )
    tile_y = send(far_packed, "y")
    tile_z = send(far_2, "back")
    tile_ring = send(far_1, "ring")
    return final(info, bands, diag, own, tile_own, far, tile_y, tile_z, tile_ring)


def solution(mesh):
    in_specs = (
        P(None, ("snap", "blk"), None),
        P("snap", None),
        P(("snap", "blk"), None),
        P(("snap", "blk")),
    )
    out_specs = P(None, None, ("snap", "blk"), None)
    return jax.shard_map(shards, mesh=mesh, in_specs=in_specs, out_specs=out_specs, check_vma=False)
```

```python
import functools
import math

import jax
import jax.numpy as jnp
from jax import lax
from jax.experimental import pallas as pl
from jax.experimental.pallas import tpu as pltpu
from jax.sharding import PartitionSpec as P

REACH = 2
OCC_STEPS = 16
SPAN = 5
LANES = 128
CHUNKS = (24, 25)
F32 = jnp.float32
BF16 = jnp.bfloat16
VMEM_BYTES = 64 * 2**20


def product(k, low, high):
    dims = (((1,), (1,)), ((), ()))
    wide = low.astype(F32)
    rows = [jnp.concatenate([(k[a][None, :] * wide[c]).astype(BF16) for a in range(3)], axis=0) for c in range(2)]
    straight = jnp.concatenate([high[0], high[1]], axis=0)
    turned = jnp.concatenate([high[1], -high[0]], axis=0)
    first = lax.dot_general(rows[0], straight, dims, preferred_element_type=F32)
    return first + lax.dot_general(rows[1], turned, dims, preferred_element_type=F32)


def weights_of(low, high, offset, scale):
    bands = low.shape[1]
    low, high = low.astype(F32), high.astype(F32)
    if isinstance(offset, int):
        flag = low[1, 0:1, bands + offset - 1 : bands + offset] if offset else 1.0
    else:
        flag = jnp.where(offset == 1, low[1, 0:1, bands : bands + 1], low[1, 0:1, bands + 1 : bands + 2])
    weights = (low[0][:, :bands] - high[1][:, :bands]) * (flag * scale)
    return jnp.concatenate([weights, weights], axis=1)


def pack(tile):
    rows = tile.shape[0]
    rest = tile[:, LANES:]
    return jnp.concatenate([tile[:, :LANES], jnp.concatenate([rest[: rows // 2], rest[rows // 2 :]], axis=1)], axis=0)


def unpack(packed):
    rows = packed.shape[0] * 2 // 3
    rest = packed[rows:]
    width = LANES // 2
    return jnp.concatenate([packed[:rows], jnp.concatenate([rest[:, :width], rest[:, width:]], axis=0)], axis=1)


OFFSETS = {"diag": (0,), "near": (1,), "far": (2, 1, 2)}


def roles(kind, info):
    first, side, core = info[0], info[1], info[2]
    if kind == "diag":
        return 0, ((0, 0),)
    if kind == "near":
        return core, ((1 - core, core),)
    pairs = ((1, 0), (jnp.where(first == 1, 3, 1), jnp.where(first == 1, 2, 3)), (0, 2))
    return side, tuple((jnp.where(side == 0, low, high), jnp.where(side == 0, high, low)) for low, high in pairs)


def pick(values, i):
    out = values[0]
    for j in range(1, len(values)):
        out = jnp.where(i == j, values[j], out)
    return out


def pair_body(kind, first_tile, tiles, plans, facts_plans, has_start, scale, info, k_hbm, *refs):
    offsets = OFFSETS[kind]
    count, blocks = len(offsets), len(plans)
    half, pairs = roles(kind, info)
    ends = facts_plans is not None
    refs = list(refs)
    take = lambda number: [refs.pop(0) for _ in range(number)]
    sources = [take(len(plan)) for plan in plans]
    facts_sources = [take(len(plan)) for plan in facts_plans] if ends else []
    start_hbm = take(1)[0] if has_start else None
    outs = take(len(refs) - 10)
    k_held, held, facts, weights, start, acc, sems, k_sem, facts_sems, start_sem = refs

    half_tiles = k_hbm.shape[1] // 2 // LANES
    first = half * half_tiles + first_tile
    k_copy = pltpu.make_async_copy(k_hbm.at[:, pl.ds(pl.multiple_of(first * LANES, LANES), tiles * LANES)], k_held, k_sem)

    def copies(plan, arrays, into, size, sems):
        out = []
        for n, (array, (where, at)) in enumerate(zip(arrays, plan)):
            when = None if where is None else info[0] == 1 if "first" in where else info[0] == 0 if "second" in where else None
            at += 0 if where is None else info[1] * half_tiles if "side" in where else info[2] * half_tiles if "core" in where else 0
            span = pl.ds(at * LANES if isinstance(at, int) else pl.multiple_of(at * LANES, LANES), size * LANES)
            out.append((when, pltpu.make_async_copy(array.at[:, :, span], into, sems.at[n])))
        return out

    def each(copies, run):
        for when, copy in copies:
            if when is None:
                run(copy)
            else:
                pl.when(when)(functools.partial(run, copy))

    begin = lambda copies: each(copies, lambda copy: copy.start())
    wait = lambda copies: each(copies, lambda copy: copy.wait())
    loads = [copies(plans[b], sources[b], held.at[b], tiles, sems.at[b]) for b in range(blocks)]
    later = []
    if ends:
        for b in range(blocks):
            later += copies(facts_plans[b], facts_sources[b], facts.at[b], 1, facts_sems.at[b])
    if has_start:
        later.append((None, pltpu.make_async_copy(start_hbm, start, start_sem)))
    begin(later)
    k_copy.start()
    for load in loads[:2]:
        begin(load)

    def order(i):
        return tuple(pick([pair[n] for pair in pairs], i) for n in (0, 1))

    wait(later)
    if ends:
        @pl.loop(0, count)
        def _(i):
            low, high = order(i)
            weights[i] = weights_of(facts[low], facts[high], 0 if kind == "diag" else pick(offsets, i), scale)

    k_copy.wait()
    wait(loads[0])

    @pl.loop(0, count)
    def _(step):
        for j in range(1, blocks):
            @pl.when(step == j - 1)
            def _():
                wait(loads[j])
                if j == 1:
                    for load in loads[2:]:
                        begin(load)

        i = pick((0, 2, 1), step) if count == 3 else step
        low, high = order(i)
        acc[i] = product(k_held[...], held[low], held[high])

    @pl.loop(0, count)
    def _(i):
        tile = acc[i]
        if has_start:
            tile = tile + start[i]
        if not ends:
            outs[0][i] = tile
            return
        tile = tile * jnp.concatenate([weights[i]] * 3, axis=0)
        if count == 1:
            outs[0][...] = tile
        else:
            @pl.when(i < 2)
            def _():
                outs[0][i] = tile

        if kind == "near":
            outs[1][...] = pack(tile).astype(BF16)
        if kind == "far":
            packed = pack(tile).astype(BF16)

            @pl.when(i != 1)
            def _():
                outs[1][i // 2] = packed

            @pl.when(i > 0)
            def _():
                outs[2][i - 1] = packed

            @pl.when(i == 1)
            def _():
                outs[3][...] = packed


def pair_sums(kind, info, k, blocks, begin, tiles, facts=None, start=None):
    bands = blocks[0][0][0].shape[1]
    count = len(OFFSETS[kind])
    ends = facts is not None
    shape = (count, 3 * bands, 2 * bands)
    arrays = lambda blocks: [part[0] for block in blocks for part in block]
    plans = lambda blocks: tuple(tuple((part[1], part[2]) for part in block) for block in blocks)
    operands = [k] + arrays(blocks) + arrays(facts or []) + ([] if start is None else [start])
    tile = shape[1:]
    packed = (9 * bands // 2, LANES)
    if not ends:
        out_shape = [jax.ShapeDtypeStruct(shape, F32)]
    elif kind == "far":
        out_shape = [jax.ShapeDtypeStruct((2, *tile), F32)] + [jax.ShapeDtypeStruct((2, *packed), BF16)] * 2
        out_shape.append(jax.ShapeDtypeStruct(packed, BF16))
    else:
        out_shape = [jax.ShapeDtypeStruct(tile, F32)] + [jax.ShapeDtypeStruct(packed, BF16)] * (kind == "near")
    return pl.pallas_call(
        functools.partial(
            pair_body, kind, begin, tiles, plans(blocks), plans(facts) if ends else None, start is not None, 1.0 / math.sqrt(k.shape[1])
        ),
        in_specs=[pl.BlockSpec(memory_space=pltpu.SMEM)] + [pl.BlockSpec(memory_space=pltpu.HBM)] * len(operands),
        out_specs=[pl.BlockSpec(memory_space=pltpu.VMEM)] * len(out_shape),
        out_shape=out_shape,
        scratch_shapes=[
            pltpu.VMEM((k.shape[0], tiles * LANES), F32),
            pltpu.VMEM((len(blocks), 2, bands, tiles * LANES), BF16),
            pltpu.VMEM((len(blocks), 2, bands, LANES), BF16),
            pltpu.VMEM((count, bands, 2 * bands), F32),
            pltpu.VMEM(shape, F32),
            pltpu.VMEM(shape, F32),
            pltpu.SemaphoreType.DMA((len(blocks), 2)),
            pltpu.SemaphoreType.DMA,
            pltpu.SemaphoreType.DMA((len(blocks), 2)),
            pltpu.SemaphoreType.DMA,
        ],
        compiler_params=pltpu.CompilerParams(vmem_limit_bytes=VMEM_BYTES),
        cost_estimate=pl.CostEstimate(flops=1000, bytes_accessed=1000, transcendentals=0),
        name=kind,
    )(info, *operands)


def mark_body(*refs):
    refs[-1][...] = jnp.zeros_like(refs[-1])


def mark(*arrays):
    return pl.pallas_call(
        mark_body,
        in_specs=[pl.BlockSpec(memory_space=pltpu.HBM)] * len(arrays),
        out_specs=pl.BlockSpec(memory_space=pltpu.VMEM),
        out_shape=jax.ShapeDtypeStruct((8, LANES), F32),
        compiler_params=pltpu.CompilerParams(vmem_limit_bytes=VMEM_BYTES),
        cost_estimate=pl.CostEstimate(flops=10**12, bytes_accessed=1000, transcendentals=0),
        name="mark",
    )(*arrays)


def pieces_body(cuts, info, levels, pairs, coeffs, *refs):
    outs, held, sems = refs[: len(cuts)], refs[-2], refs[-1]
    bands = coeffs.shape[1]
    half = coeffs.shape[2] // 2
    tiles = half // LANES
    side, core = info[1], info[2]
    span = lambda start, size: pl.ds(pl.multiple_of(start, LANES), size * LANES)
    loads, stores, at = [], [], 1
    for n, (which, start, size, more) in enumerate(cuts):
        source = half * {"y": 1 - side, "z": side, "core": 1 - core}[which] + start * LANES
        if size == 0:
            continue
        here = held.at[:, :, span(at * LANES, size)]
        loads.append(pltpu.make_async_copy(coeffs.at[:, :, span(source, size)], here, sems.at[0, n]))
        loads[-1].start()
        stores.append(pltpu.make_async_copy(here, outs[n].at[:, :, span(0, size)], sems.at[1, n]))
        at += size
    if any(more for *_, more in cuts):
        occup = levels[...].astype(F32) / OCC_STEPS
        spread = jnp.broadcast_to(occup, (bands, bands))
        lane = lax.broadcasted_iota(jnp.int32, (bands, LANES - bands), 1)
        flags = jnp.zeros((bands, LANES - bands), F32)
        for d in range(REACH):
            flags = jnp.where(lane == d, pairs[0, d].astype(F32), flags)
        held[0, :, :LANES] = jnp.concatenate([spread.T, jnp.zeros_like(flags)], axis=1).astype(BF16)
        held[1, :, :LANES] = jnp.concatenate([spread, flags], axis=1).astype(BF16)
    facts = []
    for n, (_, _, size, more) in enumerate(cuts):
        if more:
            facts.append(pltpu.make_async_copy(held.at[:, :, span(0, 1)], outs[n].at[:, :, span(size * LANES, 1)], sems.at[2, n]))
            facts[-1].start()
    for load, store in zip(loads, stores):
        load.wait()
        store.start()
    for copy in stores + facts:
        copy.wait()


def pieces(cuts, info, levels, pairs, coeffs, name):
    bands = coeffs.shape[1]
    anywhere = pl.BlockSpec(memory_space=pltpu.HBM)
    return list(
        pl.pallas_call(
            functools.partial(pieces_body, cuts),
            in_specs=[
                pl.BlockSpec(memory_space=pltpu.SMEM),
                pl.BlockSpec(memory_space=pltpu.VMEM),
                pl.BlockSpec(memory_space=pltpu.SMEM),
                anywhere,
            ],
            out_specs=[anywhere] * len(cuts),
            out_shape=[jax.ShapeDtypeStruct((2, bands, (size + int(more)) * LANES), BF16) for _, _, size, more in cuts],
            scratch_shapes=[
                pltpu.VMEM((2, bands, (1 + sum(size for _, _, size, _ in cuts)) * LANES), BF16),
                pltpu.SemaphoreType.DMA((3, len(cuts))),
            ],
            compiler_params=pltpu.CompilerParams(vmem_limit_bytes=VMEM_BYTES),
            cost_estimate=pl.CostEstimate(flops=1000, bytes_accessed=1000, transcendentals=0),
            name=name,
        )(info, levels[None, :], pairs, coeffs)
    )


def final_body(info, diag, own, core, far, up_z, across, up_y, marked, out):
    bands = out.shape[2]
    first = info[0] == 1
    low = info[1] == 0
    wide = lambda tile: unpack(tile.astype(F32))
    mine = own[...] + wide(core[...])
    middle = wide(across[...])
    near1 = jnp.where(first, mine, far[1] + middle)
    near2 = far[0] + wide(up_y[0])
    away1 = jnp.where(first, middle + wide(up_z[0]), mine)
    away2 = wide(up_y[1]) + wide(up_z[1])
    above = [jnp.where(low, near1, away1), jnp.where(low, near2, away2)]
    below = [jnp.where(low, away1, near1), jnp.where(low, away2, near2)]
    for a in range(3):
        for part in range(2):
            cut = lambda tile: tile[a * bands : (a + 1) * bands, part * bands : (part + 1) * bands]
            turn = lambda tile: -cut(tile).T if part == 0 else cut(tile).T
            out[a, part] = jnp.concatenate([turn(below[1]), turn(below[0]), cut(diag), cut(above[0]), cut(above[1])], axis=1)


def final(info, bands, *operands):
    vmem = pl.BlockSpec(memory_space=pltpu.VMEM)
    return pl.pallas_call(
        final_body,
        in_specs=[pl.BlockSpec(memory_space=pltpu.SMEM)] + [vmem] * len(operands),
        out_specs=vmem,
        out_shape=jax.ShapeDtypeStruct((3, 2, bands, SPAN * bands), F32),
        compiler_params=pltpu.CompilerParams(vmem_limit_bytes=VMEM_BYTES),
        name="final",
    )(info, *operands)


def routes(groups):
    at = lambda q, side, core: 4 * q + 2 * side + core
    away = lambda q, side: q + 1 - 2 * side
    both = [(q, side) for q in range(groups // 4) for side in (0, 1)]
    ok = [(q, s) for q, s in both if 0 <= away(q, s) < groups // 4]
    z = [(at(away(q, s), s, c), at(q, s, c)) for q, s in ok for c in (0, 1)]
    return dict(
        core=[(at(q, s, c), at(q, s, 1 - c)) for q, s in both for c in (0, 1)],
        y=[(at(q, s, c), at(q, 1 - s, c)) for q, s in both for c in (0, 1)],
        z=z,
        back=[(b, a) for a, b in z],
        across=[(at(q, s, c), at(q, 1 - s, 1 - c)) for q, s in both for c in (0, 1)],
    )


def shards(coeffs, k_plus_g, pairs, levels):
    groups = lax.axis_size("blk")
    me = lax.axis_index("blk")
    bands, plane = coeffs.shape[1:]
    tiles = plane // 2 // LANES
    core = me % 2
    side = (me // 2) % 2
    info = jnp.stack([(core == side).astype(jnp.int32), side, core])
    way = routes(groups)
    send = lambda value, name: lax.ppermute(value, "blk", way[name])
    tie = lambda *arrays: lax.optimization_barrier(arrays)

    one, two = CHUNKS
    swapped = send(coeffs, "core")
    y_one, z_one, facts = pieces(
        [("y", 0, one, False), ("z", 0, one, False), ("y", 0, 0, True)], info, levels, pairs, coeffs, "one"
    )
    facts_core = [(send(facts, "core"), None, 0)]
    coeffs, y_one, z_one = tie(coeffs, y_one, z_one)
    got_z, got_y = [send(z_one, "z")], [send(y_one, "y")]
    y_two, z_two = pieces([("y", one, two, True), ("z", one, two, True)], info, levels, pairs, coeffs, "two")
    got_z.append(send(z_two, "z"))
    got_y.append(send(y_two, "y"))
    here = [(facts, None, 0)]

    coeffs, y_two, z_two = tie(coeffs, y_two, z_two)
    (diag,) = pair_sums("diag", info, k_plus_g, [[(coeffs, None, 0)]], 0, 2 * tiles, [here])
    diag, swapped, coeffs = tie(diag, swapped, coeffs)
    own, own_packed = pair_sums(
        "near", info, k_plus_g, [[(swapped, "core", 0)], [(coeffs, "core", 0)]], 0, tiles, [facts_core, here]
    )
    tile_own = send(own_packed, "core")
    got_y[0], got_z[0], own = tie(got_y[0], got_z[0], own)
    other = [send(got_y[0], "core")]
    (sums,) = pair_sums(
        "far", info, k_plus_g, [[(got_y[0], None, 0)], [(coeffs, "side", 0)], [(got_z[0], None, 0)], [(other[0], None, 0)]], 0, one
    )
    got_y[1], sums, tile_own = tie(got_y[1], sums, tile_own)
    other.append(send(got_y[1], "core"))
    marked = mark(got_z[1])
    other[1], marked = tie(other[1], marked)
    far, pairs_02, pairs_12, pair_1 = pair_sums(
        "far", info, k_plus_g, [[(got_y[1], None, 0)], [(coeffs, "side", one)], [(got_z[1], None, 0)], [(other[1], None, 0)]], one, two,
        [[(got_y[1], None, two)], here, [(got_z[1], None, two)], [(other[1], None, two)]], sums,
    )
    tile_y = send(pairs_02, "y")
    tile_across = send(pair_1, "across")
    tile_z = send(pairs_12, "back")
    return final(info, bands, diag, own, tile_own, far, tile_z, tile_across, tile_y, marked)


def solution(mesh):
    in_specs = (
        P(None, ("snap", "blk"), None),
        P("snap", None),
        P(("snap", "blk"), None),
        P(("snap", "blk")),
    )
    out_specs = P(None, None, ("snap", "blk"), None)
    return jax.shard_map(shards, mesh=mesh, in_specs=in_specs, out_specs=out_specs, check_vma=False)
```

```python
import functools
import math

import jax
import jax.numpy as jnp
from jax import lax
from jax.experimental import pallas as pl
from jax.experimental.pallas import tpu as pltpu
from jax.sharding import PartitionSpec as P

REACH = 2
OCC_STEPS = 16
SPAN = 5
LANES = 128
CHUNKS = (13, 17, 19)
F32 = jnp.float32
BF16 = jnp.bfloat16
VMEM_BYTES = 64 * 2**20


def product(k, low, high):
    dims = (((1,), (1,)), ((), ()))
    wide = low.astype(F32)
    rows = [jnp.concatenate([(k[a][None, :] * wide[c]).astype(BF16) for a in range(3)], axis=0) for c in range(2)]
    straight = jnp.concatenate([high[0], high[1]], axis=0)
    turned = jnp.concatenate([high[1], -high[0]], axis=0)
    first = lax.dot_general(rows[0], straight, dims, preferred_element_type=F32)
    return first + lax.dot_general(rows[1], turned, dims, preferred_element_type=F32)


def weights_of(low, high, offset, scale):
    bands = low.shape[1]
    low, high = low.astype(F32), high.astype(F32)
    if isinstance(offset, int):
        flag = low[1, 0:1, bands + offset - 1 : bands + offset] if offset else 1.0
    else:
        flag = jnp.where(offset == 1, low[1, 0:1, bands : bands + 1], low[1, 0:1, bands + 1 : bands + 2])
    weights = (low[0][:, :bands] - high[1][:, :bands]) * (flag * scale)
    return jnp.concatenate([weights, weights], axis=1)


def pack(tile):
    rows = tile.shape[0]
    rest = tile[:, LANES:]
    return jnp.concatenate([tile[:, :LANES], jnp.concatenate([rest[: rows // 2], rest[rows // 2 :]], axis=1)], axis=0)


def unpack(packed):
    rows = packed.shape[0] * 2 // 3
    rest = packed[rows:]
    width = LANES // 2
    return jnp.concatenate([packed[:rows], jnp.concatenate([rest[:, :width], rest[:, width:]], axis=0)], axis=1)


OFFSETS = {"diag": (0,), "near": (1,), "far": (2, 1, 2)}


def roles(kind, info):
    first, side, core = info[0], info[1], info[2]
    if kind == "diag":
        return 0, ((0, 0),)
    if kind == "near":
        return core, ((1 - core, core),)
    pairs = ((1, 0), (jnp.where(first == 1, 3, 1), jnp.where(first == 1, 2, 3)), (0, 2))
    return side, tuple((jnp.where(side == 0, low, high), jnp.where(side == 0, high, low)) for low, high in pairs)


def position():
    me = lax.axis_index("blk")
    side, core = lax.rem(lax.div(me, 2), 2), lax.rem(me, 2)
    return jnp.where(side == core, 1, 0), side, core


def pick(values, i):
    out = values[0]
    for j in range(1, len(values)):
        out = jnp.where(i == j, values[j], out)
    return out


def pair_body(kind, first_tile, tiles, plans, facts_plans, has_start, scale, k_hbm, *refs):
    info = position()
    offsets = OFFSETS[kind]
    count, blocks = len(offsets), len(plans)
    half, pairs = roles(kind, info)
    ends = facts_plans is not None
    refs = list(refs)
    take = lambda number: [refs.pop(0) for _ in range(number)]
    sources = [take(len(plan)) for plan in plans]
    facts_sources = [take(len(plan)) for plan in facts_plans] if ends else []
    start_hbm = take(1)[0] if has_start else None
    outs = take(len(refs) - 10)
    k_held, held, facts, weights, start, acc, sems, k_sem, facts_sems, start_sem = refs

    half_tiles = k_hbm.shape[1] // 2 // LANES
    first = half * half_tiles + first_tile
    k_copy = pltpu.make_async_copy(k_hbm.at[:, pl.ds(pl.multiple_of(first * LANES, LANES), tiles * LANES)], k_held, k_sem)

    def copies(plan, arrays, into, size, sems):
        out = []
        for n, (array, (where, at)) in enumerate(zip(arrays, plan)):
            when = None if where is None else info[0] == 1 if "first" in where else info[0] == 0 if "second" in where else None
            at += 0 if where is None else info[1] * half_tiles if "side" in where else info[2] * half_tiles if "core" in where else 0
            span = pl.ds(at * LANES if isinstance(at, int) else pl.multiple_of(at * LANES, LANES), size * LANES)
            out.append((when, pltpu.make_async_copy(array.at[:, :, span], into, sems.at[n])))
        return out

    def each(copies, run):
        for when, copy in copies:
            if when is None:
                run(copy)
            else:
                pl.when(when)(functools.partial(run, copy))

    begin = lambda copies: each(copies, lambda copy: copy.start())
    wait = lambda copies: each(copies, lambda copy: copy.wait())
    loads = [copies(plans[b], sources[b], held.at[b], tiles, sems.at[b]) for b in range(blocks)]
    later = []
    if ends:
        for b in range(blocks):
            later += copies(facts_plans[b], facts_sources[b], facts.at[b], 1, facts_sems.at[b])
    if has_start:
        later.append((None, pltpu.make_async_copy(start_hbm, start, start_sem)))
    facts_copies = blocks if ends else 0
    begin(later[:facts_copies])
    k_copy.start()
    for load in loads[:2]:
        begin(load)
    begin(later[facts_copies:])

    def order(i):
        return tuple(pick([pair[n] for pair in pairs], i) for n in (0, 1))

    wait(later[:facts_copies])
    if ends:
        @pl.loop(0, count)
        def _(i):
            low, high = order(i)
            weights[i] = weights_of(facts[low], facts[high], 0 if kind == "diag" else pick(offsets, i), scale)

    k_copy.wait()
    wait(loads[0])

    @pl.loop(0, count)
    def _(step):
        for j in range(1, blocks):
            @pl.when(step == j - 1)
            def _():
                wait(loads[j])
                if j == 1:
                    for load in loads[2:]:
                        begin(load)

        i = pick((0, 2, 1), step) if count == 3 else step
        low, high = order(i)
        acc[i] = product(k_held[...], held[low], held[high])

    wait(later[facts_copies:])

    @pl.loop(0, count, unroll=True)
    def _(i):
        tile = acc[i]
        if has_start:
            tile = tile + start[i]
        if not ends:
            outs[0][i] = tile
            return
        tile = tile * jnp.concatenate([weights[i]] * 3, axis=0)
        if count == 1:
            outs[0][...] = tile
        else:
            @pl.when(i < 2)
            def _():
                outs[0][i] = tile

        if kind == "near":
            outs[1][...] = pack(tile).astype(BF16)
        if kind == "far":
            packed = pack(tile).astype(BF16)

            @pl.when(i != 1)
            def _():
                outs[1][i // 2] = packed

            @pl.when(i > 0)
            def _():
                outs[2][i - 1] = packed

            @pl.when(i == 1)
            def _():
                outs[3][...] = packed


def pair_sums(kind, k, blocks, begin, tiles, facts=None, start=None):
    bands = blocks[0][0][0].shape[1]
    count = len(OFFSETS[kind])
    ends = facts is not None
    shape = (count, 3 * bands, 2 * bands)
    arrays = lambda blocks: [part[0] for block in blocks for part in block]
    plans = lambda blocks: tuple(tuple((part[1], part[2]) for part in block) for block in blocks)
    operands = [k] + arrays(blocks) + arrays(facts or []) + ([] if start is None else [start])
    tile = shape[1:]
    packed = (9 * bands // 2, LANES)
    if not ends:
        out_shape = [jax.ShapeDtypeStruct(shape, F32)]
    elif kind == "far":
        out_shape = [jax.ShapeDtypeStruct((2, *tile), F32)] + [jax.ShapeDtypeStruct((2, *packed), BF16)] * 2
        out_shape.append(jax.ShapeDtypeStruct(packed, BF16))
    else:
        out_shape = [jax.ShapeDtypeStruct(tile, F32)] + [jax.ShapeDtypeStruct(packed, BF16)] * (kind == "near")
    return pl.pallas_call(
        functools.partial(
            pair_body, kind, begin, tiles, plans(blocks), plans(facts) if ends else None, start is not None, 1.0 / math.sqrt(k.shape[1])
        ),
        in_specs=[pl.BlockSpec(memory_space=pltpu.HBM)] * len(operands),
        out_specs=[pl.BlockSpec(memory_space=pltpu.VMEM)] * len(out_shape),
        out_shape=out_shape,
        scratch_shapes=[
            pltpu.VMEM((k.shape[0], tiles * LANES), F32),
            pltpu.VMEM((len(blocks), 2, bands, tiles * LANES), BF16),
            pltpu.VMEM((len(blocks), 2, bands, LANES), BF16),
            pltpu.VMEM((count, bands, 2 * bands), F32),
            pltpu.VMEM(shape, F32),
            pltpu.VMEM(shape, F32),
            pltpu.SemaphoreType.DMA((len(blocks), 2)),
            pltpu.SemaphoreType.DMA,
            pltpu.SemaphoreType.DMA((len(blocks), 2)),
            pltpu.SemaphoreType.DMA,
        ],
        compiler_params=pltpu.CompilerParams(vmem_limit_bytes=VMEM_BYTES),
        cost_estimate=pl.CostEstimate(flops=1000, bytes_accessed=1000, transcendentals=0),
        name=kind,
    )(*operands)


def mark_body(*refs):
    refs[-1][...] = jnp.zeros_like(refs[-1])


def mark(*arrays):
    return pl.pallas_call(
        mark_body,
        in_specs=[pl.BlockSpec(memory_space=pltpu.HBM)] * len(arrays),
        out_specs=pl.BlockSpec(memory_space=pltpu.VMEM),
        out_shape=jax.ShapeDtypeStruct((8, LANES), F32),
        compiler_params=pltpu.CompilerParams(vmem_limit_bytes=VMEM_BYTES),
        cost_estimate=pl.CostEstimate(flops=10**12, bytes_accessed=1000, transcendentals=0),
        name="mark",
    )(*arrays)


def pieces_body(cuts, levels, pairs, coeffs, *refs):
    outs, held, sems = refs[: len(cuts)], refs[-2], refs[-1]
    bands = coeffs.shape[1]
    half = coeffs.shape[2] // 2
    tiles = half // LANES
    _, side, core = position()
    span = lambda start, size: pl.ds(pl.multiple_of(start, LANES), size * LANES)
    loads, stores, at = [], [], 1
    for n, (which, start, size, more) in enumerate(cuts):
        source = half * {"y": 1 - side, "z": side, "core": 1 - core}[which] + start * LANES
        if size == 0:
            continue
        here = held.at[:, :, span(at * LANES, size)]
        loads.append(pltpu.make_async_copy(coeffs.at[:, :, span(source, size)], here, sems.at[0, n]))
        loads[-1].start()
        stores.append(pltpu.make_async_copy(here, outs[n].at[:, :, span(0, size)], sems.at[1, n]))
        at += size
    if any(more for *_, more in cuts):
        occup = levels[...].astype(F32) / OCC_STEPS
        spread = jnp.broadcast_to(occup, (bands, bands))
        lane = lax.broadcasted_iota(jnp.int32, (bands, LANES - bands), 1)
        flags = jnp.zeros((bands, LANES - bands), F32)
        for d in range(REACH):
            flags = jnp.where(lane == d, pairs[0, d].astype(F32), flags)
        held[0, :, :LANES] = jnp.concatenate([spread.T, jnp.zeros_like(flags)], axis=1).astype(BF16)
        held[1, :, :LANES] = jnp.concatenate([spread, flags], axis=1).astype(BF16)
    facts = []
    for n, (_, _, size, more) in enumerate(cuts):
        if more:
            facts.append(pltpu.make_async_copy(held.at[:, :, span(0, 1)], outs[n].at[:, :, span(size * LANES, 1)], sems.at[2, n]))
            facts[-1].start()
    for load, store in zip(loads, stores):
        load.wait()
        store.start()
    for copy in stores + facts:
        copy.wait()


def pieces(cuts, levels, pairs, coeffs, name):
    bands = coeffs.shape[1]
    anywhere = pl.BlockSpec(memory_space=pltpu.HBM)
    return list(
        pl.pallas_call(
            functools.partial(pieces_body, cuts),
            in_specs=[
                pl.BlockSpec(memory_space=pltpu.VMEM),
                pl.BlockSpec(memory_space=pltpu.SMEM),
                anywhere,
            ],
            out_specs=[anywhere] * len(cuts),
            out_shape=[jax.ShapeDtypeStruct((2, bands, (size + int(more)) * LANES), BF16) for _, _, size, more in cuts],
            scratch_shapes=[
                pltpu.VMEM((2, bands, (1 + sum(size for _, _, size, _ in cuts)) * LANES), BF16),
                pltpu.SemaphoreType.DMA((3, len(cuts))),
            ],
            compiler_params=pltpu.CompilerParams(vmem_limit_bytes=VMEM_BYTES),
            cost_estimate=pl.CostEstimate(flops=1000, bytes_accessed=1000, transcendentals=0),
            name=name,
        )(levels[None, :], pairs, coeffs)
    )


def final_body(diag, own, core, far, up_y, across, up_z, marked, result, out, sems):
    bands = out.shape[2]
    first, side, _ = position()
    first, low = first == 1, side == 0
    wide = lambda tile: unpack(tile.astype(F32))
    mine = own[...] + wide(core[...])
    middle = wide(across[...])
    near1 = jnp.where(first, mine, far[1] + middle)
    near2 = far[0] + wide(up_y[0])
    away1 = jnp.where(first, middle + wide(up_z[0]), mine)
    away2 = wide(up_y[1]) + wide(up_z[1])
    above = [jnp.where(low, near1, away1), jnp.where(low, near2, away2)]
    below = [jnp.where(low, away1, near1), jnp.where(low, away2, near2)]
    copies = []
    for a in range(3):
        for part in range(2):
            cut = lambda tile: tile[a * bands : (a + 1) * bands, part * bands : (part + 1) * bands]
            turn = lambda tile: -cut(tile).T if part == 0 else cut(tile).T
            out[a, part] = jnp.concatenate([turn(below[1]), turn(below[0]), cut(diag), cut(above[0]), cut(above[1])], axis=1)
        copies.append(pltpu.make_async_copy(out.at[a], result.at[a], sems.at[a]))
        copies[-1].start()
    for copy in copies:
        copy.wait()


def final(bands, *operands):
    vmem = pl.BlockSpec(memory_space=pltpu.VMEM)
    return pl.pallas_call(
        final_body,
        in_specs=[vmem] * len(operands),
        out_specs=pl.BlockSpec(memory_space=pltpu.HBM),
        out_shape=jax.ShapeDtypeStruct((3, 2, bands, SPAN * bands), F32),
        scratch_shapes=[pltpu.VMEM((3, 2, bands, SPAN * bands), F32), pltpu.SemaphoreType.DMA((3,))],
        compiler_params=pltpu.CompilerParams(vmem_limit_bytes=VMEM_BYTES),
        name="final",
    )(*operands)


def routes(groups):
    at = lambda q, side, core: 4 * q + 2 * side + core
    away = lambda q, side: q + 1 - 2 * side
    both = [(q, side) for q in range(groups // 4) for side in (0, 1)]
    ok = [(q, s) for q, s in both if 0 <= away(q, s) < groups // 4]
    z = [(at(away(q, s), s, c), at(q, s, c)) for q, s in ok for c in (0, 1)]
    return dict(
        core=[(at(q, s, c), at(q, s, 1 - c)) for q, s in both for c in (0, 1)],
        y=[(at(q, s, c), at(q, 1 - s, c)) for q, s in both for c in (0, 1)],
        z=z,
        back=[(b, a) for a, b in z],
        across=[(at(q, s, c), at(q, 1 - s, 1 - c)) for q, s in both for c in (0, 1)],
    )


def shards(coeffs, k_plus_g, pairs, levels):
    groups = lax.axis_size("blk")
    bands, plane = coeffs.shape[1:]
    tiles = plane // 2 // LANES
    way = routes(groups)
    send = lambda value, name: lax.ppermute(value, "blk", way[name])
    tie = lambda *arrays: lax.optimization_barrier(arrays)

    begins = [sum(CHUNKS[:i]) for i in range(len(CHUNKS))]
    last = len(CHUNKS) - 1
    swapped = send(coeffs, "core")
    y_blocks, z_blocks, facts = [[block] for block in pieces(
        [("y", 0, CHUNKS[0], False), ("z", 0, CHUNKS[0], False), ("y", 0, 0, True)], levels, pairs, coeffs, "one"
    )]
    facts = facts[0]
    here, facts_core = [(facts, None, 0)], [(send(facts, "core"), None, 0)]
    coeffs, y_blocks[0], z_blocks[0] = tie(coeffs, y_blocks[0], z_blocks[0])
    cuts = [(which, begins[i], CHUNKS[i], i == last) for i in range(1, last + 1) for which in ("y", "z")]
    blocks = pieces(cuts, levels, pairs, coeffs, "rest")
    y_blocks += blocks[0::2]
    z_blocks += blocks[1::2]
    got_y, got_z = [], []
    for y_block, z_block in zip(y_blocks, z_blocks):
        got_y.append(send(y_block, "y"))
        got_z.append(send(z_block, "z"))

    coeffs, y_blocks[-1], z_blocks[-1] = tie(coeffs, y_blocks[-1], z_blocks[-1])
    (diag,) = pair_sums("diag", k_plus_g, [[(coeffs, None, 0)]], 0, 2 * tiles, [here])
    diag, swapped, coeffs = tie(diag, swapped, coeffs)
    own, own_packed = pair_sums(
        "near", k_plus_g, [[(swapped, "core", 0)], [(coeffs, "core", 0)]], 0, tiles, [facts_core, here]
    )
    tile_own = send(own_packed, "core")
    sums, before = None, own
    for i, (begin, size) in enumerate(zip(begins, CHUNKS)):
        blocks = lambda other: [[(got_y[i], None, 0)], [(coeffs, "side", begin)], [(got_z[i], None, 0)], [(other, None, 0)]]
        if i < last:
            got_y[i], got_z[i], before = tie(got_y[i], got_z[i], before)
            if i == 0:
                own = before
            else:
                sums = before
            (sums,) = pair_sums("far", k_plus_g, blocks(send(got_y[i], "core")), begin, size, start=sums)
            before = sums
        else:
            got_y[i], sums, tile_own = tie(got_y[i], sums, tile_own)
            marked = mark(got_z[i])
            other, marked = tie(send(got_y[i], "core"), marked)
            far, pairs_02, pairs_12, pair_1 = pair_sums(
                "far", k_plus_g, blocks(other), begin, size,
                [[(got_y[i], None, size)], here, [(got_z[i], None, size)], [(other, None, size)]], sums,
            )
    tile_y = send(pairs_02, "y")
    tile_across = send(pair_1, "across")
    tile_z = send(pairs_12, "back")
    return final(bands, diag, own, tile_own, far, tile_y, tile_across, tile_z, marked)


def solution(mesh):
    in_specs = (
        P(None, ("snap", "blk"), None),
        P("snap", None),
        P(("snap", "blk"), None),
        P(("snap", "blk")),
    )
    out_specs = P(None, None, ("snap", "blk"), None)
    return jax.shard_map(shards, mesh=mesh, in_specs=in_specs, out_specs=out_specs, check_vma=False)
```

```python
import functools
import math

import jax
import jax.numpy as jnp
from jax import lax
from jax.experimental import pallas as pl
from jax.experimental.pallas import tpu as pltpu
from jax.sharding import PartitionSpec as P

REACH = 2
OCC_STEPS = 16
SPAN = 5
LANES = 128
FACTS = 16
CHUNKS = (14, 17, 18)
F32 = jnp.float32
BF16 = jnp.bfloat16
VMEM_BYTES = 64 * 2**20


def product(k, low, high):
    dims = (((1,), (1,)), ((), ()))
    wide = low.astype(F32)
    rows = [jnp.concatenate([(k[a][None, :] * wide[c]).astype(BF16) for a in range(3)], axis=0) for c in range(2)]
    straight = jnp.concatenate([high[0], high[1]], axis=0)
    turned = jnp.concatenate([high[1], -high[0]], axis=0)
    first = lax.dot_general(rows[0], straight, dims, preferred_element_type=F32)
    return first + lax.dot_general(rows[1], turned, dims, preferred_element_type=F32)


def weights_of(low, high, bands, offset, scale):
    low, high = low[0:1].astype(F32), high[0:1].astype(F32)
    if isinstance(offset, int):
        flag = low[:, bands + offset - 1 : bands + offset] if offset else 1.0
    else:
        flag = jnp.where(offset == 1, low[:, bands : bands + 1], low[:, bands + 1 : bands + 2])
    spread = lambda row: jnp.broadcast_to(row[:, :bands], (bands, bands))
    weights = (spread(low).T - spread(high)) * (flag * scale)
    return jnp.concatenate([weights, weights], axis=1)


def pack(tile):
    rows = tile.shape[0]
    rest = tile[:, LANES:]
    return jnp.concatenate([tile[:, :LANES], jnp.concatenate([rest[: rows // 2], rest[rows // 2 :]], axis=1)], axis=0)


def unpack(packed):
    rows = packed.shape[0] * 2 // 3
    rest = packed[rows:]
    width = LANES // 2
    return jnp.concatenate([packed[:rows], jnp.concatenate([rest[:, :width], rest[:, width:]], axis=0)], axis=1)


OFFSETS = {"diag": (0,), "near": (1,), "far": (2, 1, 2)}


def roles(kind, info):
    first, side, core = info[0], info[1], info[2]
    if kind == "diag":
        return 0, ((0, 0),)
    if kind == "near":
        return core, ((1 - core, core),)
    pairs = ((1, 0), (jnp.where(first == 1, 3, 1), jnp.where(first == 1, 2, 3)), (0, 2))
    return side, tuple((jnp.where(side == 0, low, high), jnp.where(side == 0, high, low)) for low, high in pairs)


def position():
    me = lax.axis_index("blk")
    side, core = lax.rem(lax.div(me, 2), 2), lax.rem(me, 2)
    return jnp.where(side == core, 1, 0), side, core


def pick(values, i):
    out = values[0]
    for j in range(1, len(values)):
        out = jnp.where(i == j, values[j], out)
    return out


def pair_body(kind, first_tile, tiles, plans, facts_plans, has_start, scale, k_hbm, *refs):
    info = position()
    offsets = OFFSETS[kind]
    count, blocks = len(offsets), len(plans)
    half, pairs = roles(kind, info)
    ends = facts_plans is not None
    refs = list(refs)
    take = lambda number: [refs.pop(0) for _ in range(number)]
    sources = [take(len(plan)) for plan in plans]
    facts_sources = [take(len(plan)) for plan in facts_plans] if ends else []
    start_hbm = take(1)[0] if has_start else None
    outs = take(len(refs) - 10)
    k_held, held, facts, weights, start, acc, sems, k_sem, facts_sems, start_sem = refs

    half_tiles = k_hbm.shape[1] // 2 // LANES
    first = half * half_tiles + first_tile
    k_copy = pltpu.make_async_copy(k_hbm.at[:, pl.ds(pl.multiple_of(first * LANES, LANES), tiles * LANES)], k_held, k_sem)

    def copies(plan, arrays, into, size, sems):
        out = []
        for n, (array, (where, at)) in enumerate(zip(arrays, plan)):
            when = None if where is None else info[0] == 1 if "first" in where else info[0] == 0 if "second" in where else None
            at += 0 if where is None else info[1] * half_tiles if "side" in where else info[2] * half_tiles if "core" in where else 0
            span = pl.ds(at * LANES if isinstance(at, int) else pl.multiple_of(at * LANES, LANES), size * LANES)
            out.append((when, pltpu.make_async_copy(array.at[:, :, span], into, sems.at[n])))
        return out

    def each(copies, run):
        for when, copy in copies:
            if when is None:
                run(copy)
            else:
                pl.when(when)(functools.partial(run, copy))

    begin = lambda copies: each(copies, lambda copy: copy.start())
    wait = lambda copies: each(copies, lambda copy: copy.wait())
    loads = [copies(plans[b], sources[b], held.at[b], tiles, sems.at[b]) for b in range(blocks)]
    later = []
    if ends:
        for b in range(blocks):
            (at,), (source,) = facts_plans[b], facts_sources[b]
            rows = source.at[pl.ds(at[1] * FACTS, FACTS)]
            later.append((None, pltpu.make_async_copy(rows, facts.at[b], facts_sems.at[b, 0])))
    if has_start:
        later.append((None, pltpu.make_async_copy(start_hbm, start, start_sem)))
    facts_copies = blocks if ends else 0
    begin(later[:facts_copies])
    k_copy.start()
    for load in loads[:2]:
        begin(load)
    begin(later[facts_copies:])

    def order(i):
        return tuple(pick([pair[n] for pair in pairs], i) for n in (0, 1))

    wait(later[:facts_copies])
    if ends:
        @pl.loop(0, count)
        def _(i):
            low, high = order(i)
            weights[i] = weights_of(facts[low], facts[high], acc.shape[2] // 2, 0 if kind == "diag" else pick(offsets, i), scale)

    k_copy.wait()
    wait(loads[0])

    @pl.loop(0, count)
    def _(step):
        for j in range(1, blocks):
            @pl.when(step == j - 1)
            def _():
                wait(loads[j])
                if j == 1:
                    for load in loads[2:]:
                        begin(load)

        i = pick((0, 2, 1), step) if count == 3 else step
        low, high = order(i)
        acc[i] = product(k_held[...], held[low], held[high])

    wait(later[facts_copies:])

    @pl.loop(0, count, unroll=True)
    def _(i):
        tile = acc[i]
        if has_start:
            tile = tile + start[i]
        if not ends:
            outs[0][i] = tile
            return
        tile = tile * jnp.concatenate([weights[i]] * 3, axis=0)
        if count == 1:
            outs[0][...] = tile
        else:
            @pl.when(i < 2)
            def _():
                outs[0][i] = tile

        if kind == "near":
            outs[1][...] = pack(tile).astype(BF16)
        if kind == "far":
            packed = pack(tile).astype(BF16)

            @pl.when(i != 1)
            def _():
                outs[1][i // 2] = packed

            @pl.when(i > 0)
            def _():
                outs[2][i - 1] = packed

            @pl.when(i == 1)
            def _():
                outs[3][...] = packed


def pair_sums(kind, k, blocks, begin, tiles, facts=None, start=None):
    bands = blocks[0][0][0].shape[1]
    count = len(OFFSETS[kind])
    ends = facts is not None
    shape = (count, 3 * bands, 2 * bands)
    arrays = lambda blocks: [part[0] for block in blocks for part in block]
    plans = lambda blocks: tuple(tuple((part[1], part[2]) for part in block) for block in blocks)
    operands = [k] + arrays(blocks) + arrays(facts or []) + ([] if start is None else [start])
    tile = shape[1:]
    packed = (9 * bands // 2, LANES)
    if not ends:
        out_shape = [jax.ShapeDtypeStruct(shape, F32)]
    elif kind == "far":
        out_shape = [jax.ShapeDtypeStruct((2, *tile), F32)] + [jax.ShapeDtypeStruct((2, *packed), BF16)] * 2
        out_shape.append(jax.ShapeDtypeStruct(packed, BF16))
    else:
        out_shape = [jax.ShapeDtypeStruct(tile, F32)] + [jax.ShapeDtypeStruct(packed, BF16)] * (kind == "near")
    return pl.pallas_call(
        functools.partial(
            pair_body, kind, begin, tiles, plans(blocks), plans(facts) if ends else None, start is not None, 1.0 / math.sqrt(k.shape[1])
        ),
        in_specs=[pl.BlockSpec(memory_space=pltpu.HBM)] * len(operands),
        out_specs=[pl.BlockSpec(memory_space=pltpu.VMEM)] * len(out_shape),
        out_shape=out_shape,
        scratch_shapes=[
            pltpu.VMEM((k.shape[0], tiles * LANES), F32),
            pltpu.VMEM((len(blocks), 2, bands, tiles * LANES), BF16),
            pltpu.VMEM((len(blocks), FACTS, LANES), BF16),
            pltpu.VMEM((count, bands, 2 * bands), F32),
            pltpu.VMEM(shape, F32),
            pltpu.VMEM(shape, F32),
            pltpu.SemaphoreType.DMA((len(blocks), 2)),
            pltpu.SemaphoreType.DMA,
            pltpu.SemaphoreType.DMA((len(blocks), 2)),
            pltpu.SemaphoreType.DMA,
        ],
        compiler_params=pltpu.CompilerParams(vmem_limit_bytes=VMEM_BYTES),
        cost_estimate=pl.CostEstimate(flops=1000, bytes_accessed=1000, transcendentals=0),
        name=kind,
    )(*operands)


def mark_body(*refs):
    refs[-1][...] = jnp.zeros_like(refs[-1])


def mark(*arrays):
    return pl.pallas_call(
        mark_body,
        in_specs=[pl.BlockSpec(memory_space=pltpu.HBM)] * len(arrays),
        out_specs=pl.BlockSpec(memory_space=pltpu.VMEM),
        out_shape=jax.ShapeDtypeStruct((8, LANES), F32),
        compiler_params=pltpu.CompilerParams(vmem_limit_bytes=VMEM_BYTES),
        cost_estimate=pl.CostEstimate(flops=10**12, bytes_accessed=1000, transcendentals=0),
        name="mark",
    )(*arrays)


def facts_body(levels, pairs, out):
    bands = levels.shape[1]
    lane = lax.broadcasted_iota(jnp.int32, (1, LANES), 1)
    row = jnp.concatenate([levels[...].astype(F32) / OCC_STEPS, jnp.zeros((1, LANES - bands), F32)], axis=1)
    for d in range(REACH):
        row = jnp.where(lane == bands + d, pairs[0, d].astype(F32), row)
    out[...] = jnp.broadcast_to(row, (FACTS, LANES)).astype(BF16)


def facts_of(levels, pairs):
    return pl.pallas_call(
        facts_body,
        in_specs=[pl.BlockSpec(memory_space=pltpu.VMEM), pl.BlockSpec(memory_space=pltpu.SMEM)],
        out_specs=pl.BlockSpec(memory_space=pltpu.VMEM),
        out_shape=jax.ShapeDtypeStruct((FACTS, LANES), BF16),
        compiler_params=pltpu.CompilerParams(vmem_limit_bytes=VMEM_BYTES),
        cost_estimate=pl.CostEstimate(flops=1000, bytes_accessed=1000, transcendentals=0),
        name="facts",
    )(levels[None, :], pairs)


def pieces_body(cuts, coeffs, *refs):
    outs, held, sems = refs[: len(cuts)], refs[-2], refs[-1]
    half = coeffs.shape[2] // 2
    _, side, _ = position()
    span = lambda start, size: pl.ds(pl.multiple_of(start, LANES), size * LANES)
    loads, stores, at = [], [], 0
    for n, (which, start, size) in enumerate(cuts):
        source = half * {"y": 1 - side, "z": side}[which] + start * LANES
        here = held.at[:, :, span(at * LANES, size)]
        loads.append(pltpu.make_async_copy(coeffs.at[:, :, span(source, size)], here, sems.at[0, n]))
        loads[-1].start()
        stores.append(pltpu.make_async_copy(here, outs[n], sems.at[1, n]))
        at += size
    for load, store in zip(loads, stores):
        load.wait()
        store.start()
    for store in stores:
        store.wait()


def pieces(cuts, coeffs, name):
    bands = coeffs.shape[1]
    anywhere = pl.BlockSpec(memory_space=pltpu.HBM)
    return list(
        pl.pallas_call(
            functools.partial(pieces_body, cuts),
            in_specs=[anywhere],
            out_specs=[anywhere] * len(cuts),
            out_shape=[jax.ShapeDtypeStruct((2, bands, size * LANES), BF16) for _, _, size in cuts],
            scratch_shapes=[
                pltpu.VMEM((2, bands, sum(size for _, _, size in cuts) * LANES), BF16),
                pltpu.SemaphoreType.DMA((2, len(cuts))),
            ],
            compiler_params=pltpu.CompilerParams(vmem_limit_bytes=VMEM_BYTES),
            cost_estimate=pl.CostEstimate(flops=1000, bytes_accessed=1000, transcendentals=0),
            name=name,
        )(coeffs)
    )


def final_body(diag, own, core, far, up_y, across, up_z, marked, result, out, sems):
    bands = out.shape[2]
    first, side, _ = position()
    first, low = first == 1, side == 0
    wide = lambda tile: unpack(tile.astype(F32))
    mine = own[...] + wide(core[...])
    middle = wide(across[...])
    near1 = jnp.where(first, mine, far[1] + middle)
    near2 = far[0] + wide(up_y[0])
    away1 = jnp.where(first, middle + wide(up_z[0]), mine)
    away2 = wide(up_y[1]) + wide(up_z[1])
    above = [jnp.where(low, near1, away1), jnp.where(low, near2, away2)]
    below = [jnp.where(low, away1, near1), jnp.where(low, away2, near2)]
    copies = []
    for a in range(3):
        for part in range(2):
            cut = lambda tile: tile[a * bands : (a + 1) * bands, part * bands : (part + 1) * bands]
            turn = lambda tile: -cut(tile).T if part == 0 else cut(tile).T
            out[a, part] = jnp.concatenate([turn(below[1]), turn(below[0]), cut(diag), cut(above[0]), cut(above[1])], axis=1)
        copies.append(pltpu.make_async_copy(out.at[a], result.at[a], sems.at[a]))
        copies[-1].start()
    for copy in copies:
        copy.wait()


def final(bands, *operands):
    vmem = pl.BlockSpec(memory_space=pltpu.VMEM)
    return pl.pallas_call(
        final_body,
        in_specs=[vmem] * len(operands),
        out_specs=pl.BlockSpec(memory_space=pltpu.HBM),
        out_shape=jax.ShapeDtypeStruct((3, 2, bands, SPAN * bands), F32),
        scratch_shapes=[pltpu.VMEM((3, 2, bands, SPAN * bands), F32), pltpu.SemaphoreType.DMA((3,))],
        compiler_params=pltpu.CompilerParams(vmem_limit_bytes=VMEM_BYTES),
        name="final",
    )(*operands)


def routes(groups):
    at = lambda q, side, core: 4 * q + 2 * side + core
    away = lambda q, side: q + 1 - 2 * side
    both = [(q, side) for q in range(groups // 4) for side in (0, 1)]
    ok = [(q, s) for q, s in both if 0 <= away(q, s) < groups // 4]
    z = [(at(away(q, s), s, c), at(q, s, c)) for q, s in ok for c in (0, 1)]
    return dict(
        core=[(at(q, s, c), at(q, s, 1 - c)) for q, s in both for c in (0, 1)],
        y=[(at(q, s, c), at(q, 1 - s, c)) for q, s in both for c in (0, 1)],
        z=z,
        back=[(b, a) for a, b in z],
        across=[(at(q, s, c), at(q, 1 - s, 1 - c)) for q, s in both for c in (0, 1)],
    )


def shards(coeffs, k_plus_g, pairs, levels):
    groups = lax.axis_size("blk")
    bands, plane = coeffs.shape[1:]
    tiles = plane // 2 // LANES
    way = routes(groups)
    send = lambda value, name: lax.ppermute(value, "blk", way[name])
    tie = lambda *arrays: lax.optimization_barrier(arrays)

    begins = [sum(CHUNKS[:i]) for i in range(len(CHUNKS))]
    last = len(CHUNKS) - 1
    half, width = tiles * LANES, CHUNKS[0] * LANES
    upper = lax.rem(lax.div(lax.axis_index("blk"), 2), 2) == 1
    low, high = coeffs[:, :, :width], coeffs[:, :, half : half + width]
    y_blocks, z_blocks = [jnp.where(upper, low, high)], [jnp.where(upper, high, low)]
    levels, coeffs, y_blocks[0], z_blocks[0] = tie(levels, coeffs, y_blocks[0], z_blocks[0])
    swapped = send(coeffs, "core")
    facts = facts_of(levels, pairs)
    coeffs, facts = tie(coeffs, facts)
    here, facts_core = [(facts, None, 0)], send(facts, "core")
    facts_y, facts_z = send(jnp.concatenate([facts, facts_core], axis=0), "y"), send(facts, "z")
    cuts = [(which, begins[i], CHUNKS[i]) for i in range(1, last + 1) for which in ("y", "z")]
    blocks = pieces(cuts, coeffs, "rest")
    y_blocks += blocks[0::2]
    z_blocks += blocks[1::2]
    got_y, got_z = [], []
    for y_block, z_block in zip(y_blocks, z_blocks):
        got_y.append(send(y_block, "y"))
        got_z.append(send(z_block, "z"))

    coeffs, y_blocks[-1], z_blocks[-1] = tie(coeffs, y_blocks[-1], z_blocks[-1])
    (diag,) = pair_sums("diag", k_plus_g, [[(coeffs, None, 0)]], 0, 2 * tiles, [here])
    diag, swapped, coeffs = tie(diag, swapped, coeffs)
    own, own_packed = pair_sums(
        "near", k_plus_g, [[(swapped, "core", 0)], [(coeffs, "core", 0)]], 0, tiles, [[(facts_core, None, 0)], here]
    )
    tile_own = send(own_packed, "core")
    sums, before = None, own
    for i, (begin, size) in enumerate(zip(begins, CHUNKS)):
        blocks = lambda other: [[(got_y[i], None, 0)], [(coeffs, "side", begin)], [(got_z[i], None, 0)], [(other, None, 0)]]
        if i < last:
            got_y[i], got_z[i], before = tie(got_y[i], got_z[i], before)
            if i == 0:
                own = before
            else:
                sums = before
            (sums,) = pair_sums("far", k_plus_g, blocks(send(got_y[i], "core")), begin, size, start=sums)
            before = sums
        else:
            got_y[i], sums, tile_own = tie(got_y[i], sums, tile_own)
            marked = mark(got_z[i], facts_y, facts_z)
            other, marked = tie(send(got_y[i], "core"), marked)
            far, pairs_02, pairs_12, pair_1 = pair_sums(
                "far", k_plus_g, blocks(other), begin, size,
                [[(facts_y, None, 0)], here, [(facts_z, None, 0)], [(facts_y, None, 1)]], sums,
            )
    tile_y = send(pairs_02, "y")
    tile_across = send(pair_1, "across")
    tile_z = send(pairs_12, "back")
    return final(bands, diag, own, tile_own, far, tile_y, tile_across, tile_z, marked)


def solution(mesh):
    in_specs = (
        P(None, ("snap", "blk"), None),
        P("snap", None),
        P(("snap", "blk"), None),
        P(("snap", "blk")),
    )
    out_specs = P(None, None, ("snap", "blk"), None)
    return jax.shard_map(shards, mesh=mesh, in_specs=in_specs, out_specs=out_specs, check_vma=False)
```

```python
import functools
import math

import jax
import jax.numpy as jnp
from jax import lax
from jax.experimental import pallas as pl
from jax.experimental.pallas import tpu as pltpu
from jax.sharding import PartitionSpec as P

REACH = 2
OCC_STEPS = 16
SPAN = 5
LANES = 128
FACTS = 16
CHUNKS = (14, 17, 18)
F32 = jnp.float32
BF16 = jnp.bfloat16
VMEM_BYTES = 64 * 2**20


def product(k, low, high):
    dims = (((1,), (1,)), ((), ()))
    wide = low.astype(F32)
    rows = [jnp.concatenate([(k[a][None, :] * wide[c]).astype(BF16) for a in range(3)], axis=0) for c in range(2)]
    straight = jnp.concatenate([high[0], high[1]], axis=0)
    turned = jnp.concatenate([high[1], -high[0]], axis=0)
    first = lax.dot_general(rows[0], straight, dims, preferred_element_type=F32)
    return first + lax.dot_general(rows[1], turned, dims, preferred_element_type=F32)


def weights_of(low, high, bands, offset, scale):
    low, high = low[0:1].astype(F32), high[0:1].astype(F32)
    if isinstance(offset, int):
        flag = low[:, bands + offset - 1 : bands + offset] if offset else 1.0
    else:
        flag = jnp.where(offset == 1, low[:, bands : bands + 1], low[:, bands + 1 : bands + 2])
    spread = lambda row: jnp.broadcast_to(row[:, :bands], (bands, bands))
    weights = (spread(low).T - spread(high)) * (flag * scale)
    return jnp.concatenate([weights, weights], axis=1)


def pack(tile):
    rows = tile.shape[0]
    rest = tile[:, LANES:]
    return jnp.concatenate([tile[:, :LANES], jnp.concatenate([rest[: rows // 2], rest[rows // 2 :]], axis=1)], axis=0)


def unpack(packed):
    rows = packed.shape[0] * 2 // 3
    rest = packed[rows:]
    width = LANES // 2
    return jnp.concatenate([packed[:rows], jnp.concatenate([rest[:, :width], rest[:, width:]], axis=0)], axis=1)


OFFSETS = {"diag": (0,), "near": (1,), "far": (2, 1, 2)}


def roles(kind, info):
    first, side, core = info[0], info[1], info[2]
    if kind == "diag":
        return 0, ((0, 0),)
    if kind == "near":
        return core, ((1 - core, core),)
    pairs = ((1, 0), (jnp.where(first == 1, 3, 1), jnp.where(first == 1, 2, 3)), (0, 2))
    return side, tuple((jnp.where(side == 0, low, high), jnp.where(side == 0, high, low)) for low, high in pairs)


def position():
    me = lax.axis_index("blk")
    side, core = lax.rem(lax.div(me, 2), 2), lax.rem(me, 2)
    return jnp.where(side == core, 1, 0), side, core


def pick(values, i):
    out = values[0]
    for j in range(1, len(values)):
        out = jnp.where(i == j, values[j], out)
    return out


def pair_body(kind, first_tile, tiles, plans, facts_plans, has_start, scale, k_hbm, *refs):
    info = position()
    offsets = OFFSETS[kind]
    count, blocks = len(offsets), len(plans)
    half, pairs = roles(kind, info)
    ends = facts_plans is not None
    refs = list(refs)
    take = lambda number: [refs.pop(0) for _ in range(number)]
    sources = [take(len(plan)) for plan in plans]
    facts_sources = [take(len(plan)) for plan in facts_plans] if ends else []
    start_hbm = take(1)[0] if has_start else None
    outs = take(len(refs) - 10)
    k_held, held, facts, weights, start, acc, sems, k_sem, facts_sems, start_sem = refs

    half_tiles = k_hbm.shape[1] // 2 // LANES
    first = half * half_tiles + first_tile
    k_copy = pltpu.make_async_copy(k_hbm.at[:, pl.ds(pl.multiple_of(first * LANES, LANES), tiles * LANES)], k_held, k_sem)

    def copies(plan, arrays, into, size, sems):
        out = []
        for n, (array, (where, at)) in enumerate(zip(arrays, plan)):
            when = None if where is None else info[0] == 1 if "first" in where else info[0] == 0 if "second" in where else None
            at += 0 if where is None else info[1] * half_tiles if "side" in where else info[2] * half_tiles if "core" in where else 0
            span = pl.ds(at * LANES if isinstance(at, int) else pl.multiple_of(at * LANES, LANES), size * LANES)
            out.append((when, pltpu.make_async_copy(array.at[:, :, span], into, sems.at[n])))
        return out

    def each(copies, run):
        for when, copy in copies:
            if when is None:
                run(copy)
            else:
                pl.when(when)(functools.partial(run, copy))

    begin = lambda copies: each(copies, lambda copy: copy.start())
    wait = lambda copies: each(copies, lambda copy: copy.wait())
    loads = [copies(plans[b], sources[b], held.at[b], tiles, sems.at[b]) for b in range(blocks)]
    later = []
    if ends:
        for b in range(blocks):
            (at,), (source,) = facts_plans[b], facts_sources[b]
            rows = source.at[pl.ds(at[1] * FACTS, FACTS)]
            later.append((None, pltpu.make_async_copy(rows, facts.at[b], facts_sems.at[b, 0])))
    if has_start:
        later.append((None, pltpu.make_async_copy(start_hbm, start, start_sem)))
    facts_copies = blocks if ends else 0
    begin(later[:facts_copies])
    k_copy.start()
    for load in loads[:2]:
        begin(load)
    begin(later[facts_copies:])

    def order(i):
        return tuple(pick([pair[n] for pair in pairs], i) for n in (0, 1))

    wait(later[:facts_copies])
    if ends:
        @pl.loop(0, count)
        def _(i):
            low, high = order(i)
            weights[i] = weights_of(facts[low], facts[high], acc.shape[2] // 2, 0 if kind == "diag" else pick(offsets, i), scale)

    k_copy.wait()
    wait(loads[0])

    @pl.loop(0, count)
    def _(step):
        for j in range(1, blocks):
            @pl.when(step == j - 1)
            def _():
                wait(loads[j])
                if j == 1:
                    for load in loads[2:]:
                        begin(load)

        i = pick((0, 2, 1), step) if count == 3 else step
        low, high = order(i)
        acc[i] = product(k_held[...], held[low], held[high])

    wait(later[facts_copies:])

    @pl.loop(0, count, unroll=True)
    def _(i):
        tile = acc[i]
        if has_start:
            tile = tile + start[i]
        if not ends:
            outs[0][i] = tile
            return
        tile = tile * jnp.concatenate([weights[i]] * 3, axis=0)
        if count == 1:
            outs[0][...] = tile
        else:
            @pl.when(i < 2)
            def _():
                outs[0][i] = tile

        if kind == "near":
            outs[1][...] = pack(tile).astype(BF16)
        if kind == "far":
            packed = pack(tile).astype(BF16)

            @pl.when(i != 1)
            def _():
                outs[1][i // 2] = packed

            @pl.when(i > 0)
            def _():
                outs[2][i - 1] = packed

            @pl.when(i == 1)
            def _():
                outs[3][...] = packed


def pair_sums(kind, k, blocks, begin, tiles, facts=None, start=None):
    bands = blocks[0][0][0].shape[1]
    count = len(OFFSETS[kind])
    ends = facts is not None
    shape = (count, 3 * bands, 2 * bands)
    arrays = lambda blocks: [part[0] for block in blocks for part in block]
    plans = lambda blocks: tuple(tuple((part[1], part[2]) for part in block) for block in blocks)
    operands = [k] + arrays(blocks) + arrays(facts or []) + ([] if start is None else [start])
    tile = shape[1:]
    packed = (9 * bands // 2, LANES)
    if not ends:
        out_shape = [jax.ShapeDtypeStruct(shape, F32)]
    elif kind == "far":
        out_shape = [jax.ShapeDtypeStruct((2, *tile), F32)] + [jax.ShapeDtypeStruct((2, *packed), BF16)] * 2
        out_shape.append(jax.ShapeDtypeStruct(packed, BF16))
    else:
        out_shape = [jax.ShapeDtypeStruct(tile, F32)] + [jax.ShapeDtypeStruct(packed, BF16)] * (kind == "near")
    return pl.pallas_call(
        functools.partial(
            pair_body, kind, begin, tiles, plans(blocks), plans(facts) if ends else None, start is not None, 1.0 / math.sqrt(k.shape[1])
        ),
        in_specs=[pl.BlockSpec(memory_space=pltpu.HBM)] * len(operands),
        out_specs=[pl.BlockSpec(memory_space=pltpu.VMEM)] * len(out_shape),
        out_shape=out_shape,
        scratch_shapes=[
            pltpu.VMEM((k.shape[0], tiles * LANES), F32),
            pltpu.VMEM((len(blocks), 2, bands, tiles * LANES), BF16),
            pltpu.VMEM((len(blocks), FACTS, LANES), BF16),
            pltpu.VMEM((count, bands, 2 * bands), F32),
            pltpu.VMEM(shape, F32),
            pltpu.VMEM(shape, F32),
            pltpu.SemaphoreType.DMA((len(blocks), 2)),
            pltpu.SemaphoreType.DMA,
            pltpu.SemaphoreType.DMA((len(blocks), 2)),
            pltpu.SemaphoreType.DMA,
        ],
        compiler_params=pltpu.CompilerParams(vmem_limit_bytes=VMEM_BYTES),
        cost_estimate=pl.CostEstimate(flops=1000, bytes_accessed=1000, transcendentals=0),
        name=kind,
    )(*operands)


def mark_body(*refs):
    refs[-1][...] = jnp.zeros_like(refs[-1])


def mark(*arrays):
    return pl.pallas_call(
        mark_body,
        in_specs=[pl.BlockSpec(memory_space=pltpu.HBM)] * len(arrays),
        out_specs=pl.BlockSpec(memory_space=pltpu.VMEM),
        out_shape=jax.ShapeDtypeStruct((8, LANES), F32),
        compiler_params=pltpu.CompilerParams(vmem_limit_bytes=VMEM_BYTES),
        cost_estimate=pl.CostEstimate(flops=10**12, bytes_accessed=1000, transcendentals=0),
        name="mark",
    )(*arrays)


def facts_body(levels, pairs, out):
    bands = levels.shape[1]
    lane = lax.broadcasted_iota(jnp.int32, (1, LANES), 1)
    row = jnp.concatenate([levels[...].astype(F32) / OCC_STEPS, jnp.zeros((1, LANES - bands), F32)], axis=1)
    for d in range(REACH):
        row = jnp.where(lane == bands + d, pairs[0, d].astype(F32), row)
    out[...] = jnp.broadcast_to(row, (FACTS, LANES)).astype(BF16)


def facts_of(levels, pairs):
    return pl.pallas_call(
        facts_body,
        in_specs=[pl.BlockSpec(memory_space=pltpu.VMEM), pl.BlockSpec(memory_space=pltpu.SMEM)],
        out_specs=pl.BlockSpec(memory_space=pltpu.VMEM),
        out_shape=jax.ShapeDtypeStruct((FACTS, LANES), BF16),
        compiler_params=pltpu.CompilerParams(vmem_limit_bytes=VMEM_BYTES),
        cost_estimate=pl.CostEstimate(flops=1000, bytes_accessed=1000, transcendentals=0),
        name="facts",
    )(levels[None, :], pairs)


def pieces_body(cuts, coeffs, *refs):
    outs, held, sems = refs[: len(cuts)], refs[-2], refs[-1]
    half = coeffs.shape[2] // 2
    _, side, _ = position()
    span = lambda start, size: pl.ds(pl.multiple_of(start, LANES), size * LANES)
    loads, stores, at = [], [], 0
    for n, (which, start, size) in enumerate(cuts):
        source = half * {"y": 1 - side, "z": side}[which] + start * LANES
        here = held.at[:, :, span(at * LANES, size)]
        loads.append(pltpu.make_async_copy(coeffs.at[:, :, span(source, size)], here, sems.at[0, n]))
        loads[-1].start()
        stores.append(pltpu.make_async_copy(here, outs[n], sems.at[1, n]))
        at += size
    for load, store in zip(loads, stores):
        load.wait()
        store.start()
    for store in stores:
        store.wait()


def pieces(cuts, coeffs, name):
    bands = coeffs.shape[1]
    anywhere = pl.BlockSpec(memory_space=pltpu.HBM)
    return list(
        pl.pallas_call(
            functools.partial(pieces_body, cuts),
            in_specs=[anywhere],
            out_specs=[anywhere] * len(cuts),
            out_shape=[jax.ShapeDtypeStruct((2, bands, size * LANES), BF16) for _, _, size in cuts],
            scratch_shapes=[
                pltpu.VMEM((2, bands, sum(size for _, _, size in cuts) * LANES), BF16),
                pltpu.SemaphoreType.DMA((2, len(cuts))),
            ],
            compiler_params=pltpu.CompilerParams(vmem_limit_bytes=VMEM_BYTES),
            cost_estimate=pl.CostEstimate(flops=1000, bytes_accessed=1000, transcendentals=0),
            name=name,
        )(coeffs)
    )


def final_body(diag, own, core, far, up_y, across, up_z, marked, result, out, sems):
    bands = out.shape[2]
    first, side, _ = position()
    first, low = first == 1, side == 0
    wide = lambda tile: unpack(tile.astype(F32))
    mine = own[...] + wide(core[...])
    middle = wide(across[...])
    near1 = jnp.where(first, mine, far[1] + middle)
    near2 = far[0] + wide(up_y[0])
    away1 = jnp.where(first, middle + wide(up_z[0]), mine)
    away2 = wide(up_y[1]) + wide(up_z[1])
    above = [jnp.where(low, near1, away1), jnp.where(low, near2, away2)]
    below = [jnp.where(low, away1, near1), jnp.where(low, away2, near2)]
    copies = []
    for a in range(3):
        for part in range(2):
            cut = lambda tile: tile[a * bands : (a + 1) * bands, part * bands : (part + 1) * bands]
            turn = lambda tile: -cut(tile).T if part == 0 else cut(tile).T
            out[a, part] = jnp.concatenate([turn(below[1]), turn(below[0]), cut(diag), cut(above[0]), cut(above[1])], axis=1)
        copies.append(pltpu.make_async_copy(out.at[a], result.at[a], sems.at[a]))
        copies[-1].start()
    for copy in copies:
        copy.wait()


def final(bands, *operands):
    vmem = pl.BlockSpec(memory_space=pltpu.VMEM)
    return pl.pallas_call(
        final_body,
        in_specs=[vmem] * len(operands),
        out_specs=pl.BlockSpec(memory_space=pltpu.HBM),
        out_shape=jax.ShapeDtypeStruct((3, 2, bands, SPAN * bands), F32),
        scratch_shapes=[pltpu.VMEM((3, 2, bands, SPAN * bands), F32), pltpu.SemaphoreType.DMA((3,))],
        compiler_params=pltpu.CompilerParams(vmem_limit_bytes=VMEM_BYTES),
        name="final",
    )(*operands)


def routes(groups):
    at = lambda q, side, core: 4 * q + 2 * side + core
    away = lambda q, side: q + 1 - 2 * side
    both = [(q, side) for q in range(groups // 4) for side in (0, 1)]
    ok = [(q, s) for q, s in both if 0 <= away(q, s) < groups // 4]
    z = [(at(away(q, s), s, c), at(q, s, c)) for q, s in ok for c in (0, 1)]
    return dict(
        core=[(at(q, s, c), at(q, s, 1 - c)) for q, s in both for c in (0, 1)],
        y=[(at(q, s, c), at(q, 1 - s, c)) for q, s in both for c in (0, 1)],
        z=z,
        back=[(b, a) for a, b in z],
        across=[(at(q, s, c), at(q, 1 - s, 1 - c)) for q, s in both for c in (0, 1)],
    )


def shards(coeffs, k_plus_g, pairs, levels):
    groups = lax.axis_size("blk")
    bands, plane = coeffs.shape[1:]
    tiles = plane // 2 // LANES
    way = routes(groups)
    send = lambda value, name: lax.ppermute(value, "blk", way[name])
    tie = lambda *arrays: lax.optimization_barrier(arrays)

    begins = [sum(CHUNKS[:i]) for i in range(len(CHUNKS))]
    last = len(CHUNKS) - 1
    y_blocks, z_blocks = [[block] for block in pieces([("y", 0, CHUNKS[0]), ("z", 0, CHUNKS[0])], coeffs, "one")]
    levels, coeffs, y_blocks[0], z_blocks[0] = tie(levels, coeffs, y_blocks[0], z_blocks[0])
    swapped = send(coeffs, "core")
    facts = facts_of(levels, pairs)
    coeffs, facts = tie(coeffs, facts)
    here, facts_core = [(facts, None, 0)], send(facts, "core")
    facts_y, facts_z = send(jnp.concatenate([facts, facts_core], axis=0), "y"), send(facts, "z")
    cuts = [(which, begins[i], CHUNKS[i]) for i in range(1, last + 1) for which in ("y", "z")]
    blocks = pieces(cuts, coeffs, "rest")
    y_blocks += blocks[0::2]
    z_blocks += blocks[1::2]
    got_y, got_z = [], []
    for y_block, z_block in zip(y_blocks, z_blocks):
        got_y.append(send(y_block, "y"))
        got_z.append(send(z_block, "z"))

    coeffs, y_blocks[-1], z_blocks[-1] = tie(coeffs, y_blocks[-1], z_blocks[-1])
    (diag,) = pair_sums("diag", k_plus_g, [[(coeffs, None, 0)]], 0, 2 * tiles, [here])
    diag, swapped, coeffs = tie(diag, swapped, coeffs)
    own, own_packed = pair_sums(
        "near", k_plus_g, [[(swapped, "core", 0)], [(coeffs, "core", 0)]], 0, tiles, [[(facts_core, None, 0)], here]
    )
    tile_own = send(own_packed, "core")
    sums, before = None, own
    for i, (begin, size) in enumerate(zip(begins, CHUNKS)):
        blocks = lambda other: [[(got_y[i], None, 0)], [(coeffs, "side", begin)], [(got_z[i], None, 0)], [(other, None, 0)]]
        if i < last:
            got_y[i], got_z[i], before = tie(got_y[i], got_z[i], before)
            if i == 0:
                own = before
            else:
                sums = before
            (sums,) = pair_sums("far", k_plus_g, blocks(send(got_y[i], "core")), begin, size, start=sums)
            before = sums
        else:
            got_y[i], sums, tile_own = tie(got_y[i], sums, tile_own)
            marked = mark(got_z[i], facts_y, facts_z)
            other, marked = tie(send(got_y[i], "core"), marked)
            far, pairs_02, pairs_12, pair_1 = pair_sums(
                "far", k_plus_g, blocks(other), begin, size,
                [[(facts_y, None, 0)], here, [(facts_z, None, 0)], [(facts_y, None, 1)]], sums,
            )
    tile_y = send(pairs_02, "y")
    tile_across = send(pair_1, "across")
    tile_z = send(pairs_12, "back")
    return final(bands, diag, own, tile_own, far, tile_y, tile_across, tile_z, marked)


def solution(mesh):
    in_specs = (
        P(None, ("snap", "blk"), None),
        P("snap", None),
        P(("snap", "blk"), None),
        P(("snap", "blk")),
    )
    out_specs = P(None, None, ("snap", "blk"), None)
    return jax.shard_map(shards, mesh=mesh, in_specs=in_specs, out_specs=out_specs, check_vma=False)
```

```python
import functools
import math

import jax
import jax.numpy as jnp
from jax import lax
from jax.experimental import pallas as pl
from jax.experimental.pallas import tpu as pltpu
from jax.sharding import PartitionSpec as P

REACH = 2
OCC_STEPS = 16
SPAN = 5
LANES = 128
FACTS = 16
CHUNKS = (14, 17, 18)
F32 = jnp.float32
BF16 = jnp.bfloat16
VMEM_BYTES = 64 * 2**20


def product(k, low, high):
    dims = (((1,), (1,)), ((), ()))
    wide = low.astype(F32)
    rows = [jnp.concatenate([(k[a][None, :] * wide[c]).astype(BF16) for a in range(3)], axis=0) for c in range(2)]
    straight = jnp.concatenate([high[0], high[1]], axis=0)
    turned = jnp.concatenate([high[1], -high[0]], axis=0)
    first = lax.dot_general(rows[0], straight, dims, preferred_element_type=F32)
    return first + lax.dot_general(rows[1], turned, dims, preferred_element_type=F32)


def weights_of(low, high, bands, offset, scale):
    low, high = low[0:1].astype(F32), high[0:1].astype(F32)
    if isinstance(offset, int):
        flag = low[:, bands + offset - 1 : bands + offset] if offset else 1.0
    else:
        flag = jnp.where(offset == 1, low[:, bands : bands + 1], low[:, bands + 1 : bands + 2])
    spread = lambda row: jnp.broadcast_to(row[:, :bands], (bands, bands))
    weights = (spread(low).T - spread(high)) * (flag * scale)
    return jnp.concatenate([weights, weights], axis=1)


def pack(tile):
    rows = tile.shape[0]
    rest = tile[:, LANES:]
    return jnp.concatenate([tile[:, :LANES], jnp.concatenate([rest[: rows // 2], rest[rows // 2 :]], axis=1)], axis=0)


def unpack(packed):
    rows = packed.shape[0] * 2 // 3
    rest = packed[rows:]
    width = LANES // 2
    return jnp.concatenate([packed[:rows], jnp.concatenate([rest[:, :width], rest[:, width:]], axis=0)], axis=1)


OFFSETS = {"diag": (0,), "near": (1,), "far": (2, 1, 2)}


def roles(kind, info):
    first, side, core = info[0], info[1], info[2]
    if kind == "diag":
        return 0, ((0, 0),)
    if kind == "near":
        return core, ((1 - core, core),)
    pairs = ((1, 0), (jnp.where(first == 1, 3, 1), jnp.where(first == 1, 2, 3)), (0, 2))
    return side, tuple((jnp.where(side == 0, low, high), jnp.where(side == 0, high, low)) for low, high in pairs)


def position():
    me = lax.axis_index("blk")
    side, core = lax.rem(lax.div(me, 2), 2), lax.rem(me, 2)
    return jnp.where(side == core, 1, 0), side, core


def pick(values, i):
    out = values[0]
    for j in range(1, len(values)):
        out = jnp.where(i == j, values[j], out)
    return out


def pair_body(kind, first_tile, tiles, plans, facts_plans, has_start, scale, k_hbm, *refs):
    info = position()
    offsets = OFFSETS[kind]
    count, blocks = len(offsets), len(plans)
    half, pairs = roles(kind, info)
    ends = facts_plans is not None
    refs = list(refs)
    take = lambda number: [refs.pop(0) for _ in range(number)]
    sources = [take(len(plan)) for plan in plans]
    facts_sources = [take(len(plan)) for plan in facts_plans] if ends else []
    start_hbm = take(1)[0] if has_start else None
    outs = take(len(refs) - 10)
    k_held, held, facts, weights, start, acc, sems, k_sem, facts_sems, start_sem = refs

    half_tiles = k_hbm.shape[1] // 2 // LANES
    first = half * half_tiles + first_tile
    k_copy = pltpu.make_async_copy(k_hbm.at[:, pl.ds(pl.multiple_of(first * LANES, LANES), tiles * LANES)], k_held, k_sem)

    def copies(plan, arrays, into, size, sems):
        out = []
        for n, (array, (where, at)) in enumerate(zip(arrays, plan)):
            when = None if where is None else info[0] == 1 if "first" in where else info[0] == 0 if "second" in where else None
            at += 0 if where is None else info[1] * half_tiles if "side" in where else info[2] * half_tiles if "core" in where else 0
            span = pl.ds(at * LANES if isinstance(at, int) else pl.multiple_of(at * LANES, LANES), size * LANES)
            out.append((when, pltpu.make_async_copy(array.at[:, :, span], into, sems.at[n])))
        return out

    def each(copies, run):
        for when, copy in copies:
            if when is None:
                run(copy)
            else:
                pl.when(when)(functools.partial(run, copy))

    begin = lambda copies: each(copies, lambda copy: copy.start())
    wait = lambda copies: each(copies, lambda copy: copy.wait())
    loads = [copies(plans[b], sources[b], held.at[b], tiles, sems.at[b]) for b in range(blocks)]
    later = []
    if ends:
        for b in range(blocks):
            (at,), (source,) = facts_plans[b], facts_sources[b]
            rows = source.at[pl.ds(at[1] * FACTS, FACTS)]
            later.append((None, pltpu.make_async_copy(rows, facts.at[b], facts_sems.at[b, 0])))
    if has_start:
        later.append((None, pltpu.make_async_copy(start_hbm, start, start_sem)))
    facts_copies = blocks if ends else 0
    begin(later[:facts_copies])
    k_copy.start()
    for load in loads[:2]:
        begin(load)
    begin(later[facts_copies:])

    def order(i):
        return tuple(pick([pair[n] for pair in pairs], i) for n in (0, 1))

    wait(later[:facts_copies])
    if ends:
        @pl.loop(0, count)
        def _(i):
            low, high = order(i)
            weights[i] = weights_of(facts[low], facts[high], acc.shape[2] // 2, 0 if kind == "diag" else pick(offsets, i), scale)

    k_copy.wait()
    wait(loads[0])

    @pl.loop(0, count)
    def _(step):
        for j in range(1, blocks):
            @pl.when(step == j - 1)
            def _():
                wait(loads[j])
                if j == 1:
                    for load in loads[2:]:
                        begin(load)

        i = pick((0, 2, 1), step) if count == 3 else step
        low, high = order(i)
        acc[i] = product(k_held[...], held[low], held[high])

    wait(later[facts_copies:])

    @pl.loop(0, count, unroll=True)
    def _(i):
        tile = acc[i]
        if has_start:
            tile = tile + start[i]
        if not ends:
            outs[0][i] = tile
            return
        tile = tile * jnp.concatenate([weights[i]] * 3, axis=0)
        if count == 1:
            outs[0][...] = tile
        else:
            @pl.when(i < 2)
            def _():
                outs[0][i] = tile

        if kind == "near":
            outs[1][...] = pack(tile).astype(BF16)
        if kind == "far":
            packed = pack(tile).astype(BF16)

            @pl.when(i != 1)
            def _():
                outs[1][i // 2] = packed

            @pl.when(i > 0)
            def _():
                outs[2][i - 1] = packed

            @pl.when(i == 1)
            def _():
                outs[3][...] = packed


def pair_sums(kind, k, blocks, begin, tiles, facts=None, start=None):
    bands = blocks[0][0][0].shape[1]
    count = len(OFFSETS[kind])
    ends = facts is not None
    shape = (count, 3 * bands, 2 * bands)
    arrays = lambda blocks: [part[0] for block in blocks for part in block]
    plans = lambda blocks: tuple(tuple((part[1], part[2]) for part in block) for block in blocks)
    operands = [k] + arrays(blocks) + arrays(facts or []) + ([] if start is None else [start])
    tile = shape[1:]
    packed = (9 * bands // 2, LANES)
    if not ends:
        out_shape = [jax.ShapeDtypeStruct(shape, F32)]
    elif kind == "far":
        out_shape = [jax.ShapeDtypeStruct((2, *tile), F32)] + [jax.ShapeDtypeStruct((2, *packed), BF16)] * 2
        out_shape.append(jax.ShapeDtypeStruct(packed, BF16))
    else:
        out_shape = [jax.ShapeDtypeStruct(tile, F32)] + [jax.ShapeDtypeStruct(packed, BF16)] * (kind == "near")
    return pl.pallas_call(
        functools.partial(
            pair_body, kind, begin, tiles, plans(blocks), plans(facts) if ends else None, start is not None, 1.0 / math.sqrt(k.shape[1])
        ),
        in_specs=[pl.BlockSpec(memory_space=pltpu.HBM)] * len(operands),
        out_specs=[pl.BlockSpec(memory_space=pltpu.VMEM)] * len(out_shape),
        out_shape=out_shape,
        scratch_shapes=[
            pltpu.VMEM((k.shape[0], tiles * LANES), F32),
            pltpu.VMEM((len(blocks), 2, bands, tiles * LANES), BF16),
            pltpu.VMEM((len(blocks), FACTS, LANES), BF16),
            pltpu.VMEM((count, bands, 2 * bands), F32),
            pltpu.VMEM(shape, F32),
            pltpu.VMEM(shape, F32),
            pltpu.SemaphoreType.DMA((len(blocks), 2)),
            pltpu.SemaphoreType.DMA,
            pltpu.SemaphoreType.DMA((len(blocks), 2)),
            pltpu.SemaphoreType.DMA,
        ],
        compiler_params=pltpu.CompilerParams(vmem_limit_bytes=VMEM_BYTES),
        cost_estimate=pl.CostEstimate(flops=1000, bytes_accessed=1000, transcendentals=0),
        name=kind,
    )(*operands)


def mark_body(*refs):
    refs[-1][...] = jnp.zeros_like(refs[-1])


def mark(*arrays):
    return pl.pallas_call(
        mark_body,
        in_specs=[pl.BlockSpec(memory_space=pltpu.HBM)] * len(arrays),
        out_specs=pl.BlockSpec(memory_space=pltpu.VMEM),
        out_shape=jax.ShapeDtypeStruct((8, LANES), F32),
        compiler_params=pltpu.CompilerParams(vmem_limit_bytes=VMEM_BYTES),
        cost_estimate=pl.CostEstimate(flops=10**12, bytes_accessed=1000, transcendentals=0),
        name="mark",
    )(*arrays)


def facts_body(levels, pairs, out):
    bands = levels.shape[1]
    lane = lax.broadcasted_iota(jnp.int32, (1, LANES), 1)
    row = jnp.concatenate([levels[...].astype(F32) / OCC_STEPS, jnp.zeros((1, LANES - bands), F32)], axis=1)
    for d in range(REACH):
        row = jnp.where(lane == bands + d, pairs[0, d].astype(F32), row)
    out[...] = jnp.broadcast_to(row, (FACTS, LANES)).astype(BF16)


def facts_of(levels, pairs):
    return pl.pallas_call(
        facts_body,
        in_specs=[pl.BlockSpec(memory_space=pltpu.VMEM), pl.BlockSpec(memory_space=pltpu.SMEM)],
        out_specs=pl.BlockSpec(memory_space=pltpu.VMEM),
        out_shape=jax.ShapeDtypeStruct((FACTS, LANES), BF16),
        compiler_params=pltpu.CompilerParams(vmem_limit_bytes=VMEM_BYTES),
        cost_estimate=pl.CostEstimate(flops=1000, bytes_accessed=1000, transcendentals=0),
        name="facts",
    )(levels[None, :], pairs)


def pieces_body(cuts, coeffs, *refs):
    outs, held, sems = refs[: len(cuts)], refs[-2], refs[-1]
    half = coeffs.shape[2] // 2
    _, side, _ = position()
    span = lambda start, size: pl.ds(pl.multiple_of(start, LANES), size * LANES)
    loads, stores, at = [], [], 0
    for n, (which, start, size) in enumerate(cuts):
        source = half * {"y": 1 - side, "z": side}[which] + start * LANES
        here = held.at[:, :, span(at * LANES, size)]
        loads.append(pltpu.make_async_copy(coeffs.at[:, :, span(source, size)], here, sems.at[0, n]))
        loads[-1].start()
        stores.append(pltpu.make_async_copy(here, outs[n], sems.at[1, n]))
        at += size
    for load, store in zip(loads, stores):
        load.wait()
        store.start()
    for store in stores:
        store.wait()


def pieces(cuts, coeffs, name):
    bands = coeffs.shape[1]
    anywhere = pl.BlockSpec(memory_space=pltpu.HBM)
    return list(
        pl.pallas_call(
            functools.partial(pieces_body, cuts),
            in_specs=[anywhere],
            out_specs=[anywhere] * len(cuts),
            out_shape=[jax.ShapeDtypeStruct((2, bands, size * LANES), BF16) for _, _, size in cuts],
            scratch_shapes=[
                pltpu.VMEM((2, bands, sum(size for _, _, size in cuts) * LANES), BF16),
                pltpu.SemaphoreType.DMA((2, len(cuts))),
            ],
            compiler_params=pltpu.CompilerParams(vmem_limit_bytes=VMEM_BYTES),
            cost_estimate=pl.CostEstimate(flops=1000, bytes_accessed=1000, transcendentals=0),
            name=name,
        )(coeffs)
    )


def final_body(diag, own, core, far, up_y, across, up_z, marked, result, out, sems):
    bands = out.shape[2]
    first, side, _ = position()
    first, low = first == 1, side == 0
    wide = lambda tile: unpack(tile.astype(F32))
    mine = own[...] + wide(core[...])
    middle = wide(across[...])
    near1 = jnp.where(first, mine, far[1] + middle)
    near2 = far[0] + wide(up_y[0])
    away1 = jnp.where(first, middle + wide(up_z[0]), mine)
    away2 = wide(up_y[1]) + wide(up_z[1])
    above = [jnp.where(low, near1, away1), jnp.where(low, near2, away2)]
    below = [jnp.where(low, away1, near1), jnp.where(low, away2, near2)]
    copies = []
    for a in range(3):
        rows = slice(a * bands, (a + 1) * bands)
        turned = [tile[rows].T for tile in (below[1], below[0])]
        for part in range(2):
            span = slice(part * bands, (part + 1) * bands)
            mirrored = [-tile[span] if part == 0 else tile[span] for tile in turned]
            straight = [tile[rows, span] for tile in (diag, *above)]
            out[a, part] = jnp.concatenate(mirrored + straight, axis=1)
        copies.append(pltpu.make_async_copy(out.at[a], result.at[a], sems.at[a]))
        copies[-1].start()
    for copy in copies:
        copy.wait()


def final(bands, *operands):
    vmem = pl.BlockSpec(memory_space=pltpu.VMEM)
    return pl.pallas_call(
        final_body,
        in_specs=[vmem] * len(operands),
        out_specs=pl.BlockSpec(memory_space=pltpu.HBM),
        out_shape=jax.ShapeDtypeStruct((3, 2, bands, SPAN * bands), F32),
        scratch_shapes=[pltpu.VMEM((3, 2, bands, SPAN * bands), F32), pltpu.SemaphoreType.DMA((3,))],
        compiler_params=pltpu.CompilerParams(vmem_limit_bytes=VMEM_BYTES),
        name="final",
    )(*operands)


def routes(groups):
    at = lambda q, side, core: 4 * q + 2 * side + core
    away = lambda q, side: q + 1 - 2 * side
    both = [(q, side) for q in range(groups // 4) for side in (0, 1)]
    ok = [(q, s) for q, s in both if 0 <= away(q, s) < groups // 4]
    z = [(at(away(q, s), s, c), at(q, s, c)) for q, s in ok for c in (0, 1)]
    return dict(
        core=[(at(q, s, c), at(q, s, 1 - c)) for q, s in both for c in (0, 1)],
        y=[(at(q, s, c), at(q, 1 - s, c)) for q, s in both for c in (0, 1)],
        z=z,
        back=[(b, a) for a, b in z],
        across=[(at(q, s, c), at(q, 1 - s, 1 - c)) for q, s in both for c in (0, 1)],
    )


def shards(coeffs, k_plus_g, pairs, levels):
    groups = lax.axis_size("blk")
    bands, plane = coeffs.shape[1:]
    tiles = plane // 2 // LANES
    way = routes(groups)
    send = lambda value, name: lax.ppermute(value, "blk", way[name])
    tie = lambda *arrays: lax.optimization_barrier(arrays)

    begins = [sum(CHUNKS[:i]) for i in range(len(CHUNKS))]
    last = len(CHUNKS) - 1
    y_blocks, z_blocks = [[block] for block in pieces([("y", 0, CHUNKS[0]), ("z", 0, CHUNKS[0])], coeffs, "one")]
    levels, coeffs, y_blocks[0], z_blocks[0] = tie(levels, coeffs, y_blocks[0], z_blocks[0])
    swapped = send(coeffs, "core")
    facts = facts_of(levels, pairs)
    coeffs, facts = tie(coeffs, facts)
    here, facts_core = [(facts, None, 0)], send(facts, "core")
    facts_y, facts_z = send(jnp.concatenate([facts, facts_core], axis=0), "y"), send(facts, "z")
    cuts = [(which, begins[i], CHUNKS[i]) for i in range(1, last + 1) for which in ("y", "z")]
    blocks = pieces(cuts, coeffs, "rest")
    y_blocks += blocks[0::2]
    z_blocks += blocks[1::2]
    got_y, got_z = [], []
    for y_block, z_block in zip(y_blocks, z_blocks):
        got_y.append(send(y_block, "y"))
        got_z.append(send(z_block, "z"))

    coeffs, y_blocks[-1], z_blocks[-1] = tie(coeffs, y_blocks[-1], z_blocks[-1])
    (diag,) = pair_sums("diag", k_plus_g, [[(coeffs, None, 0)]], 0, 2 * tiles, [here])
    diag, swapped, coeffs = tie(diag, swapped, coeffs)
    own, own_packed = pair_sums(
        "near", k_plus_g, [[(swapped, "core", 0)], [(coeffs, "core", 0)]], 0, tiles, [[(facts_core, None, 0)], here]
    )
    tile_own = send(own_packed, "core")
    sums, before = None, own
    for i, (begin, size) in enumerate(zip(begins, CHUNKS)):
        blocks = lambda other: [[(got_y[i], None, 0)], [(coeffs, "side", begin)], [(got_z[i], None, 0)], [(other, None, 0)]]
        if i < last:
            got_y[i], got_z[i], before = tie(got_y[i], got_z[i], before)
            if i == 0:
                own = before
            else:
                sums = before
            (sums,) = pair_sums("far", k_plus_g, blocks(send(got_y[i], "core")), begin, size, start=sums)
            before = sums
        else:
            got_y[i], sums, tile_own = tie(got_y[i], sums, tile_own)
            marked = mark(got_z[i], facts_y, facts_z)
            other, marked = tie(send(got_y[i], "core"), marked)
            far, pairs_02, pairs_12, pair_1 = pair_sums(
                "far", k_plus_g, blocks(other), begin, size,
                [[(facts_y, None, 0)], here, [(facts_z, None, 0)], [(facts_y, None, 1)]], sums,
            )
    tile_y = send(pairs_02, "y")
    tile_across = send(pair_1, "across")
    tile_z = send(pairs_12, "back")
    return final(bands, diag, own, tile_own, far, tile_y, tile_across, tile_z, marked)


def solution(mesh):
    in_specs = (
        P(None, ("snap", "blk"), None),
        P("snap", None),
        P(("snap", "blk"), None),
        P(("snap", "blk")),
    )
    out_specs = P(None, None, ("snap", "blk"), None)
    return jax.shard_map(shards, mesh=mesh, in_specs=in_specs, out_specs=out_specs, check_vma=False)
```

```python
import functools
import math

import jax
import jax.numpy as jnp
from jax import lax
from jax.experimental import pallas as pl
from jax.experimental.pallas import tpu as pltpu
from jax.sharding import PartitionSpec as P

REACH = 2
OCC_STEPS = 16
SPAN = 5
LANES = 128
FACTS = 16
CHUNKS = (14, 17, 18)
F32 = jnp.float32
BF16 = jnp.bfloat16
VMEM_BYTES = 64 * 2**20


def product(k, low, high):
    dims = (((1,), (1,)), ((), ()))
    wide = low.astype(F32)
    rows = [jnp.concatenate([(k[a][None, :] * wide[c]).astype(BF16) for a in range(3)], axis=0) for c in range(2)]
    straight = jnp.concatenate([high[0], high[1]], axis=0)
    turned = jnp.concatenate([high[1], -high[0]], axis=0)
    first = lax.dot_general(rows[0], straight, dims, preferred_element_type=F32)
    return first + lax.dot_general(rows[1], turned, dims, preferred_element_type=F32)


def weights_of(low, high, bands, offset, scale):
    low, high = low[0:1].astype(F32), high[0:1].astype(F32)
    if isinstance(offset, int):
        flag = low[:, bands + offset - 1 : bands + offset] if offset else 1.0
    else:
        flag = jnp.where(offset == 1, low[:, bands : bands + 1], low[:, bands + 1 : bands + 2])
    spread = lambda row: jnp.broadcast_to(row[:, :bands], (bands, bands))
    weights = (spread(low).T - spread(high)) * (flag * scale)
    return jnp.concatenate([weights, weights], axis=1)


def pack(tile):
    rows = tile.shape[0]
    rest = tile[:, LANES:]
    return jnp.concatenate([tile[:, :LANES], jnp.concatenate([rest[: rows // 2], rest[rows // 2 :]], axis=1)], axis=0)


def unpack(packed):
    rows = packed.shape[0] * 2 // 3
    rest = packed[rows:]
    width = LANES // 2
    return jnp.concatenate([packed[:rows], jnp.concatenate([rest[:, :width], rest[:, width:]], axis=0)], axis=1)


OFFSETS = {"diag": (0,), "near": (1,), "far": (2, 1, 2)}


def roles(kind, info):
    first, side, core = info[0], info[1], info[2]
    if kind == "diag":
        return 0, ((0, 0),)
    if kind == "near":
        return core, ((1 - core, core),)
    pairs = ((1, 0), (jnp.where(first == 1, 3, 1), jnp.where(first == 1, 2, 3)), (0, 2))
    return side, tuple((jnp.where(side == 0, low, high), jnp.where(side == 0, high, low)) for low, high in pairs)


def position():
    me = lax.axis_index("blk")
    side, core = lax.rem(lax.div(me, 2), 2), lax.rem(me, 2)
    return jnp.where(side == core, 1, 0), side, core


def pick(values, i):
    out = values[0]
    for j in range(1, len(values)):
        out = jnp.where(i == j, values[j], out)
    return out


def pair_body(kind, first_tile, tiles, plans, facts_plans, has_start, scale, k_hbm, *refs):
    info = position()
    offsets = OFFSETS[kind]
    count, blocks = len(offsets), len(plans)
    half, pairs = roles(kind, info)
    ends = facts_plans is not None
    refs = list(refs)
    take = lambda number: [refs.pop(0) for _ in range(number)]
    sources = [take(len(plan)) for plan in plans]
    facts_sources = [take(len(plan)) for plan in facts_plans] if ends else []
    start_hbm = take(1)[0] if has_start else None
    outs = take(len(refs) - 10)
    k_held, held, facts, weights, start, acc, sems, k_sem, facts_sems, start_sem = refs

    half_tiles = k_hbm.shape[1] // 2 // LANES
    first = half * half_tiles + first_tile
    k_copy = pltpu.make_async_copy(k_hbm.at[:, pl.ds(pl.multiple_of(first * LANES, LANES), tiles * LANES)], k_held, k_sem)

    def copies(plan, arrays, into, size, sems):
        out = []
        for n, (array, (where, at)) in enumerate(zip(arrays, plan)):
            when = None if where is None else info[0] == 1 if "first" in where else info[0] == 0 if "second" in where else None
            at += 0 if where is None else info[1] * half_tiles if "side" in where else info[2] * half_tiles if "core" in where else 0
            span = pl.ds(at * LANES if isinstance(at, int) else pl.multiple_of(at * LANES, LANES), size * LANES)
            out.append((when, pltpu.make_async_copy(array.at[:, :, span], into, sems.at[n])))
        return out

    def each(copies, run):
        for when, copy in copies:
            if when is None:
                run(copy)
            else:
                pl.when(when)(functools.partial(run, copy))

    begin = lambda copies: each(copies, lambda copy: copy.start())
    wait = lambda copies: each(copies, lambda copy: copy.wait())
    loads = [copies(plans[b], sources[b], held.at[b], tiles, sems.at[b]) for b in range(blocks)]
    later = []
    if ends:
        for b in range(blocks):
            (at,), (source,) = facts_plans[b], facts_sources[b]
            rows = source.at[pl.ds(at[1] * FACTS, FACTS)]
            later.append((None, pltpu.make_async_copy(rows, facts.at[b], facts_sems.at[b, 0])))
    if has_start:
        later.append((None, pltpu.make_async_copy(start_hbm, start, start_sem)))
    facts_copies = blocks if ends else 0
    begin(later[:facts_copies])
    k_copy.start()
    for load in loads[:2]:
        begin(load)
    begin(later[facts_copies:])

    def order(i):
        return tuple(pick([pair[n] for pair in pairs], i) for n in (0, 1))

    wait(later[:facts_copies])
    if ends:
        @pl.loop(0, count)
        def _(i):
            low, high = order(i)
            weights[i] = weights_of(facts[low], facts[high], acc.shape[2] // 2, 0 if kind == "diag" else pick(offsets, i), scale)

    k_copy.wait()
    wait(loads[0])

    @pl.loop(0, count)
    def _(step):
        for j in range(1, blocks):
            @pl.when(step == j - 1)
            def _():
                wait(loads[j])
                if j == 1:
                    for load in loads[2:]:
                        begin(load)

        i = pick((0, 2, 1), step) if count == 3 else step
        low, high = order(i)
        acc[i] = product(k_held[...], held[low], held[high])

    wait(later[facts_copies:])

    @pl.loop(0, count, unroll=True)
    def _(i):
        tile = acc[i]
        if has_start:
            tile = tile + start[i]
        if not ends:
            outs[0][i] = tile
            return
        tile = tile * jnp.concatenate([weights[i]] * 3, axis=0)
        if count == 1:
            outs[0][...] = tile
        else:
            @pl.when(i < 2)
            def _():
                outs[0][i] = tile

        if kind == "near":
            outs[1][...] = pack(tile).astype(BF16)
        if kind == "far":
            packed = pack(tile).astype(BF16)

            @pl.when(i != 1)
            def _():
                outs[1][i // 2] = packed

            @pl.when(i > 0)
            def _():
                outs[2][i - 1] = packed

            @pl.when(i == 1)
            def _():
                outs[3][...] = packed


def pair_sums(kind, k, blocks, begin, tiles, facts=None, start=None):
    bands = blocks[0][0][0].shape[1]
    count = len(OFFSETS[kind])
    ends = facts is not None
    shape = (count, 3 * bands, 2 * bands)
    arrays = lambda blocks: [part[0] for block in blocks for part in block]
    plans = lambda blocks: tuple(tuple((part[1], part[2]) for part in block) for block in blocks)
    operands = [k] + arrays(blocks) + arrays(facts or []) + ([] if start is None else [start])
    tile = shape[1:]
    packed = (9 * bands // 2, LANES)
    if not ends:
        out_shape = [jax.ShapeDtypeStruct(shape, F32)]
    elif kind == "far":
        out_shape = [jax.ShapeDtypeStruct((2, *tile), F32)] + [jax.ShapeDtypeStruct((2, *packed), BF16)] * 2
        out_shape.append(jax.ShapeDtypeStruct(packed, BF16))
    else:
        out_shape = [jax.ShapeDtypeStruct(tile, F32)] + [jax.ShapeDtypeStruct(packed, BF16)] * (kind == "near")
    return pl.pallas_call(
        functools.partial(
            pair_body, kind, begin, tiles, plans(blocks), plans(facts) if ends else None, start is not None, 1.0 / math.sqrt(k.shape[1])
        ),
        in_specs=[pl.BlockSpec(memory_space=pltpu.HBM)] * len(operands),
        out_specs=[pl.BlockSpec(memory_space=pltpu.VMEM)] * len(out_shape),
        out_shape=out_shape,
        scratch_shapes=[
            pltpu.VMEM((k.shape[0], tiles * LANES), F32),
            pltpu.VMEM((len(blocks), 2, bands, tiles * LANES), BF16),
            pltpu.VMEM((len(blocks), FACTS, LANES), BF16),
            pltpu.VMEM((count, bands, 2 * bands), F32),
            pltpu.VMEM(shape, F32),
            pltpu.VMEM(shape, F32),
            pltpu.SemaphoreType.DMA((len(blocks), 2)),
            pltpu.SemaphoreType.DMA,
            pltpu.SemaphoreType.DMA((len(blocks), 2)),
            pltpu.SemaphoreType.DMA,
        ],
        compiler_params=pltpu.CompilerParams(vmem_limit_bytes=VMEM_BYTES),
        cost_estimate=pl.CostEstimate(flops=1000, bytes_accessed=1000, transcendentals=0),
        name=kind,
    )(*operands)


def mark_body(*refs):
    refs[-1][...] = jnp.zeros_like(refs[-1])


def mark(*arrays):
    return pl.pallas_call(
        mark_body,
        in_specs=[pl.BlockSpec(memory_space=pltpu.HBM)] * len(arrays),
        out_specs=pl.BlockSpec(memory_space=pltpu.VMEM),
        out_shape=jax.ShapeDtypeStruct((8, LANES), F32),
        compiler_params=pltpu.CompilerParams(vmem_limit_bytes=VMEM_BYTES),
        cost_estimate=pl.CostEstimate(flops=10**12, bytes_accessed=1000, transcendentals=0),
        name="mark",
    )(*arrays)


def facts_body(levels, pairs, out):
    bands = levels.shape[1]
    lane = lax.broadcasted_iota(jnp.int32, (1, LANES), 1)
    row = jnp.concatenate([levels[...].astype(F32) / OCC_STEPS, jnp.zeros((1, LANES - bands), F32)], axis=1)
    for d in range(REACH):
        row = jnp.where(lane == bands + d, pairs[0, d].astype(F32), row)
    out[...] = jnp.broadcast_to(row, (FACTS, LANES)).astype(BF16)


def facts_of(levels, pairs):
    return pl.pallas_call(
        facts_body,
        in_specs=[pl.BlockSpec(memory_space=pltpu.VMEM), pl.BlockSpec(memory_space=pltpu.SMEM)],
        out_specs=pl.BlockSpec(memory_space=pltpu.VMEM),
        out_shape=jax.ShapeDtypeStruct((FACTS, LANES), BF16),
        compiler_params=pltpu.CompilerParams(vmem_limit_bytes=VMEM_BYTES),
        cost_estimate=pl.CostEstimate(flops=1000, bytes_accessed=1000, transcendentals=0),
        name="facts",
    )(levels[None, :], pairs)


def pieces_body(cuts, coeffs, *refs):
    outs, held, sems = refs[: len(cuts)], refs[-2], refs[-1]
    half = coeffs.shape[2] // 2
    _, side, _ = position()
    span = lambda start, size: pl.ds(pl.multiple_of(start, LANES), size * LANES)
    loads, stores, at = [], [], 0
    for n, (which, start, size) in enumerate(cuts):
        source = half * {"y": 1 - side, "z": side}[which] + start * LANES
        here = held.at[:, :, span(at * LANES, size)]
        for part in range(2):
            loads.append(pltpu.make_async_copy(coeffs.at[part, :, span(source, size)], here.at[part], sems.at[0, n, part]))
            loads[-1].start()
            stores.append(pltpu.make_async_copy(here.at[part], outs[n].at[part], sems.at[1, n, part]))
        at += size
    for load, store in zip(loads, stores):
        load.wait()
        store.start()
    for store in stores:
        store.wait()


def pieces(cuts, coeffs, name):
    bands = coeffs.shape[1]
    anywhere = pl.BlockSpec(memory_space=pltpu.HBM)
    return list(
        pl.pallas_call(
            functools.partial(pieces_body, cuts),
            in_specs=[anywhere],
            out_specs=[anywhere] * len(cuts),
            out_shape=[jax.ShapeDtypeStruct((2, bands, size * LANES), BF16) for _, _, size in cuts],
            scratch_shapes=[
                pltpu.VMEM((2, bands, sum(size for _, _, size in cuts) * LANES), BF16),
                pltpu.SemaphoreType.DMA((2, len(cuts), 2)),
            ],
            compiler_params=pltpu.CompilerParams(vmem_limit_bytes=VMEM_BYTES),
            cost_estimate=pl.CostEstimate(flops=1000, bytes_accessed=1000, transcendentals=0),
            name=name,
        )(coeffs)
    )


def final_body(diag, own, core, far, up_y, across, up_z, marked, result, out, sems):
    bands = out.shape[2]
    first, side, _ = position()
    first, low = first == 1, side == 0
    wide = lambda tile: unpack(tile.astype(F32))
    mine = own[...] + wide(core[...])
    middle = wide(across[...])
    near1 = jnp.where(first, mine, far[1] + middle)
    near2 = far[0] + wide(up_y[0])
    away1 = jnp.where(first, middle + wide(up_z[0]), mine)
    away2 = wide(up_y[1]) + wide(up_z[1])
    above = [jnp.where(low, near1, away1), jnp.where(low, near2, away2)]
    below = [jnp.where(low, away1, near1), jnp.where(low, away2, near2)]
    copies = []
    for a in range(3):
        rows = slice(a * bands, (a + 1) * bands)
        turned = [tile[rows].T for tile in (below[1], below[0])]
        for part in range(2):
            span = slice(part * bands, (part + 1) * bands)
            mirrored = [-tile[span] if part == 0 else tile[span] for tile in turned]
            straight = [tile[rows, span] for tile in (diag, *above)]
            out[a, part] = jnp.concatenate(mirrored + straight, axis=1)
        copies.append(pltpu.make_async_copy(out.at[a], result.at[a], sems.at[a]))
        copies[-1].start()
    for copy in copies:
        copy.wait()


def final(bands, *operands):
    vmem = pl.BlockSpec(memory_space=pltpu.VMEM)
    return pl.pallas_call(
        final_body,
        in_specs=[vmem] * len(operands),
        out_specs=pl.BlockSpec(memory_space=pltpu.HBM),
        out_shape=jax.ShapeDtypeStruct((3, 2, bands, SPAN * bands), F32),
        scratch_shapes=[pltpu.VMEM((3, 2, bands, SPAN * bands), F32), pltpu.SemaphoreType.DMA((3,))],
        compiler_params=pltpu.CompilerParams(vmem_limit_bytes=VMEM_BYTES),
        name="final",
    )(*operands)


def routes(groups):
    at = lambda q, side, core: 4 * q + 2 * side + core
    away = lambda q, side: q + 1 - 2 * side
    both = [(q, side) for q in range(groups // 4) for side in (0, 1)]
    ok = [(q, s) for q, s in both if 0 <= away(q, s) < groups // 4]
    z = [(at(away(q, s), s, c), at(q, s, c)) for q, s in ok for c in (0, 1)]
    return dict(
        core=[(at(q, s, c), at(q, s, 1 - c)) for q, s in both for c in (0, 1)],
        y=[(at(q, s, c), at(q, 1 - s, c)) for q, s in both for c in (0, 1)],
        z=z,
        back=[(b, a) for a, b in z],
        across=[(at(q, s, c), at(q, 1 - s, 1 - c)) for q, s in both for c in (0, 1)],
    )


def shards(coeffs, k_plus_g, pairs, levels):
    groups = lax.axis_size("blk")
    bands, plane = coeffs.shape[1:]
    tiles = plane // 2 // LANES
    way = routes(groups)
    send = lambda value, name: lax.ppermute(value, "blk", way[name])
    tie = lambda *arrays: lax.optimization_barrier(arrays)

    begins = [sum(CHUNKS[:i]) for i in range(len(CHUNKS))]
    last = len(CHUNKS) - 1
    y_blocks, z_blocks = [[block] for block in pieces([("y", 0, CHUNKS[0]), ("z", 0, CHUNKS[0])], coeffs, "one")]
    levels, coeffs, y_blocks[0], z_blocks[0] = tie(levels, coeffs, y_blocks[0], z_blocks[0])
    swapped = send(coeffs, "core")
    facts = facts_of(levels, pairs)
    coeffs, facts = tie(coeffs, facts)
    here, facts_core = [(facts, None, 0)], send(facts, "core")
    facts_y, facts_z = send(jnp.concatenate([facts, facts_core], axis=0), "y"), send(facts, "z")
    cuts = [(which, begins[i], CHUNKS[i]) for i in range(1, last + 1) for which in ("y", "z")]
    blocks = pieces(cuts, coeffs, "rest")
    y_blocks += blocks[0::2]
    z_blocks += blocks[1::2]
    got_y, got_z = [], []
    for y_block, z_block in zip(y_blocks, z_blocks):
        got_y.append(send(y_block, "y"))
        got_z.append(send(z_block, "z"))

    coeffs, y_blocks[-1], z_blocks[-1] = tie(coeffs, y_blocks[-1], z_blocks[-1])
    (diag,) = pair_sums("diag", k_plus_g, [[(coeffs, None, 0)]], 0, 2 * tiles, [here])
    diag, swapped, coeffs = tie(diag, swapped, coeffs)
    own, own_packed = pair_sums(
        "near", k_plus_g, [[(swapped, "core", 0)], [(coeffs, "core", 0)]], 0, tiles, [[(facts_core, None, 0)], here]
    )
    tile_own = send(own_packed, "core")
    sums, before = None, own
    for i, (begin, size) in enumerate(zip(begins, CHUNKS)):
        blocks = lambda other: [[(got_y[i], None, 0)], [(coeffs, "side", begin)], [(got_z[i], None, 0)], [(other, None, 0)]]
        if i < last:
            got_y[i], got_z[i], before = tie(got_y[i], got_z[i], before)
            if i == 0:
                own = before
            else:
                sums = before
            (sums,) = pair_sums("far", k_plus_g, blocks(send(got_y[i], "core")), begin, size, start=sums)
            before = sums
        else:
            got_y[i], sums, tile_own = tie(got_y[i], sums, tile_own)
            marked = mark(got_z[i], facts_y, facts_z)
            other, marked = tie(send(got_y[i], "core"), marked)
            far, pairs_02, pairs_12, pair_1 = pair_sums(
                "far", k_plus_g, blocks(other), begin, size,
                [[(facts_y, None, 0)], here, [(facts_z, None, 0)], [(facts_y, None, 1)]], sums,
            )
    tile_y = send(pairs_02, "y")
    tile_across = send(pair_1, "across")
    tile_z = send(pairs_12, "back")
    return final(bands, diag, own, tile_own, far, tile_y, tile_across, tile_z, marked)


def solution(mesh):
    in_specs = (
        P(None, ("snap", "blk"), None),
        P("snap", None),
        P(("snap", "blk"), None),
        P(("snap", "blk")),
    )
    out_specs = P(None, None, ("snap", "blk"), None)
    return jax.shard_map(shards, mesh=mesh, in_specs=in_specs, out_specs=out_specs, check_vma=False)
```

```python
import functools
import math

import jax
import jax.numpy as jnp
from jax import lax
from jax.experimental import pallas as pl
from jax.experimental.pallas import tpu as pltpu
from jax.sharding import PartitionSpec as P

REACH = 2
OCC_STEPS = 16
SPAN = 5
LANES = 128
FACTS = 16
CHUNKS = (14, 17, 18)
F32 = jnp.float32
BF16 = jnp.bfloat16
VMEM_BYTES = 64 * 2**20


def product(k, low, high):
    dims = (((1,), (1,)), ((), ()))
    wide = low.astype(F32)
    rows = [jnp.concatenate([(k[a][None, :] * wide[c]).astype(BF16) for a in range(3)], axis=0) for c in range(2)]
    straight = jnp.concatenate([high[0], high[1]], axis=0)
    turned = jnp.concatenate([high[1], -high[0]], axis=0)
    first = lax.dot_general(rows[0], straight, dims, preferred_element_type=F32)
    return first + lax.dot_general(rows[1], turned, dims, preferred_element_type=F32)


def weights_of(low, high, bands, offset, scale):
    low, high = low[0:1].astype(F32), high[0:1].astype(F32)
    if isinstance(offset, int):
        flag = low[:, bands + offset - 1 : bands + offset] if offset else 1.0
    else:
        flag = jnp.where(offset == 1, low[:, bands : bands + 1], low[:, bands + 1 : bands + 2])
    spread = lambda row: jnp.broadcast_to(row[:, :bands], (bands, bands))
    weights = (spread(low).T - spread(high)) * (flag * scale)
    return jnp.concatenate([weights, weights], axis=1)


def pack(tile):
    rows = tile.shape[0]
    rest = tile[:, LANES:]
    return jnp.concatenate([tile[:, :LANES], jnp.concatenate([rest[: rows // 2], rest[rows // 2 :]], axis=1)], axis=0)


def unpack(packed):
    rows = packed.shape[0] * 2 // 3
    rest = packed[rows:]
    width = LANES // 2
    return jnp.concatenate([packed[:rows], jnp.concatenate([rest[:, :width], rest[:, width:]], axis=0)], axis=1)


OFFSETS = {"diag": (0,), "near": (1,), "far": (2, 1, 2)}


def roles(kind, info):
    first, side, core = info[0], info[1], info[2]
    if kind == "diag":
        return 0, ((0, 0),)
    if kind == "near":
        return core, ((1 - core, core),)
    pairs = ((1, 0), (jnp.where(first == 1, 3, 1), jnp.where(first == 1, 2, 3)), (0, 2))
    return side, tuple((jnp.where(side == 0, low, high), jnp.where(side == 0, high, low)) for low, high in pairs)


def position():
    me = lax.axis_index("blk")
    side, core = lax.rem(lax.div(me, 2), 2), lax.rem(me, 2)
    return jnp.where(side == core, 1, 0), side, core


def pick(values, i):
    out = values[0]
    for j in range(1, len(values)):
        out = jnp.where(i == j, values[j], out)
    return out


def pair_body(kind, first_tile, tiles, plans, facts_plans, has_start, scale, k_hbm, *refs):
    info = position()
    offsets = OFFSETS[kind]
    count, blocks = len(offsets), len(plans)
    half, pairs = roles(kind, info)
    ends = facts_plans is not None
    refs = list(refs)
    take = lambda number: [refs.pop(0) for _ in range(number)]
    sources = [take(len(plan)) for plan in plans]
    facts_sources = [take(len(plan)) for plan in facts_plans] if ends else []
    start_hbm = take(1)[0] if has_start else None
    outs = take(len(refs) - 10)
    k_held, held, facts, weights, start, acc, sems, k_sem, facts_sems, start_sem = refs

    half_tiles = k_hbm.shape[1] // 2 // LANES
    first = half * half_tiles + first_tile
    k_copy = pltpu.make_async_copy(k_hbm.at[:, pl.ds(pl.multiple_of(first * LANES, LANES), tiles * LANES)], k_held, k_sem)

    def copies(plan, arrays, into, size, sems):
        out = []
        for n, (array, (where, at)) in enumerate(zip(arrays, plan)):
            when = None if where is None else info[0] == 1 if "first" in where else info[0] == 0 if "second" in where else None
            at += 0 if where is None else info[1] * half_tiles if "side" in where else info[2] * half_tiles if "core" in where else 0
            span = pl.ds(at * LANES if isinstance(at, int) else pl.multiple_of(at * LANES, LANES), size * LANES)
            out.append((when, pltpu.make_async_copy(array.at[:, :, span], into, sems.at[n])))
        return out

    def each(copies, run):
        for when, copy in copies:
            if when is None:
                run(copy)
            else:
                pl.when(when)(functools.partial(run, copy))

    begin = lambda copies: each(copies, lambda copy: copy.start())
    wait = lambda copies: each(copies, lambda copy: copy.wait())
    loads = [copies(plans[b], sources[b], held.at[b], tiles, sems.at[b]) for b in range(blocks)]
    later = []
    if ends:
        for b in range(blocks):
            (at,), (source,) = facts_plans[b], facts_sources[b]
            rows = source.at[pl.ds(at[1] * FACTS, FACTS)]
            later.append((None, pltpu.make_async_copy(rows, facts.at[b], facts_sems.at[b, 0])))
    if has_start:
        later.append((None, pltpu.make_async_copy(start_hbm, start, start_sem)))
    facts_copies = blocks if ends else 0
    begin(later[:facts_copies])
    k_copy.start()
    for load in loads[:2]:
        begin(load)
    begin(later[facts_copies:])

    def order(i):
        return tuple(pick([pair[n] for pair in pairs], i) for n in (0, 1))

    wait(later[:facts_copies])
    if ends:
        @pl.loop(0, count)
        def _(i):
            low, high = order(i)
            weights[i] = weights_of(facts[low], facts[high], acc.shape[2] // 2, 0 if kind == "diag" else pick(offsets, i), scale)

    k_copy.wait()
    wait(loads[0])

    @pl.loop(0, count)
    def _(step):
        for j in range(1, blocks):
            @pl.when(step == j - 1)
            def _():
                wait(loads[j])
                if j == 1:
                    for load in loads[2:]:
                        begin(load)

        i = pick((0, 2, 1), step) if count == 3 else step
        low, high = order(i)
        acc[i] = product(k_held[...], held[low], held[high])

    wait(later[facts_copies:])

    @pl.loop(0, count, unroll=True)
    def _(i):
        tile = acc[i]
        if has_start:
            tile = tile + start[i]
        if not ends:
            outs[0][i] = tile
            return
        tile = tile * jnp.concatenate([weights[i]] * 3, axis=0)
        if count == 1:
            outs[0][...] = tile
        if kind == "near":
            outs[1][...] = pack(tile).astype(BF16)
        if kind == "far":
            packed = pack(tile).astype(BF16)

            @pl.when(i != 1)
            def _():
                outs[0][i // 2] = packed

            @pl.when(i > 0)
            def _():
                outs[1][i - 1] = packed

            @pl.when(i == 1)
            def _():
                outs[2][...] = packed


def pair_sums(kind, k, blocks, begin, tiles, facts=None, start=None):
    bands = blocks[0][0][0].shape[1]
    count = len(OFFSETS[kind])
    ends = facts is not None
    shape = (count, 3 * bands, 2 * bands)
    arrays = lambda blocks: [part[0] for block in blocks for part in block]
    plans = lambda blocks: tuple(tuple((part[1], part[2]) for part in block) for block in blocks)
    operands = [k] + arrays(blocks) + arrays(facts or []) + ([] if start is None else [start])
    tile = shape[1:]
    packed = (9 * bands // 2, LANES)
    if not ends:
        out_shape = [jax.ShapeDtypeStruct(shape, F32)]
    elif kind == "far":
        out_shape = [jax.ShapeDtypeStruct((2, *packed), BF16)] * 2
        out_shape.append(jax.ShapeDtypeStruct(packed, BF16))
    else:
        out_shape = [jax.ShapeDtypeStruct(tile, F32)] + [jax.ShapeDtypeStruct(packed, BF16)] * (kind == "near")
    return pl.pallas_call(
        functools.partial(
            pair_body, kind, begin, tiles, plans(blocks), plans(facts) if ends else None, start is not None, 1.0 / math.sqrt(k.shape[1])
        ),
        in_specs=[pl.BlockSpec(memory_space=pltpu.HBM)] * len(operands),
        out_specs=[pl.BlockSpec(memory_space=pltpu.VMEM)] * len(out_shape),
        out_shape=out_shape,
        scratch_shapes=[
            pltpu.VMEM((k.shape[0], tiles * LANES), F32),
            pltpu.VMEM((len(blocks), 2, bands, tiles * LANES), BF16),
            pltpu.VMEM((len(blocks), FACTS, LANES), BF16),
            pltpu.VMEM((count, bands, 2 * bands), F32),
            pltpu.VMEM(shape, F32),
            pltpu.VMEM(shape, F32),
            pltpu.SemaphoreType.DMA((len(blocks), 2)),
            pltpu.SemaphoreType.DMA,
            pltpu.SemaphoreType.DMA((len(blocks), 2)),
            pltpu.SemaphoreType.DMA,
        ],
        compiler_params=pltpu.CompilerParams(vmem_limit_bytes=VMEM_BYTES),
        cost_estimate=pl.CostEstimate(flops=1000, bytes_accessed=1000, transcendentals=0),
        name=kind,
    )(*operands)


def mark_body(*refs):
    refs[-1][...] = jnp.zeros_like(refs[-1])


def mark(*arrays):
    return pl.pallas_call(
        mark_body,
        in_specs=[pl.BlockSpec(memory_space=pltpu.HBM)] * len(arrays),
        out_specs=pl.BlockSpec(memory_space=pltpu.VMEM),
        out_shape=jax.ShapeDtypeStruct((8, LANES), F32),
        compiler_params=pltpu.CompilerParams(vmem_limit_bytes=VMEM_BYTES),
        cost_estimate=pl.CostEstimate(flops=10**12, bytes_accessed=1000, transcendentals=0),
        name="mark",
    )(*arrays)


def facts_body(levels, pairs, out):
    bands = levels.shape[1]
    lane = lax.broadcasted_iota(jnp.int32, (1, LANES), 1)
    row = jnp.concatenate([levels[...].astype(F32) / OCC_STEPS, jnp.zeros((1, LANES - bands), F32)], axis=1)
    for d in range(REACH):
        row = jnp.where(lane == bands + d, pairs[0, d].astype(F32), row)
    out[...] = jnp.broadcast_to(row, (FACTS, LANES)).astype(BF16)


def facts_of(levels, pairs):
    return pl.pallas_call(
        facts_body,
        in_specs=[pl.BlockSpec(memory_space=pltpu.VMEM), pl.BlockSpec(memory_space=pltpu.SMEM)],
        out_specs=pl.BlockSpec(memory_space=pltpu.VMEM),
        out_shape=jax.ShapeDtypeStruct((FACTS, LANES), BF16),
        compiler_params=pltpu.CompilerParams(vmem_limit_bytes=VMEM_BYTES),
        cost_estimate=pl.CostEstimate(flops=1000, bytes_accessed=1000, transcendentals=0),
        name="facts",
    )(levels[None, :], pairs)


def pieces_body(cuts, coeffs, *refs):
    outs, held, sems = refs[: len(cuts)], refs[-2], refs[-1]
    half = coeffs.shape[2] // 2
    _, side, _ = position()
    span = lambda start, size: pl.ds(pl.multiple_of(start, LANES), size * LANES)
    loads, stores, at = [], [], 0
    for n, (which, start, size) in enumerate(cuts):
        source = half * {"y": 1 - side, "z": side}[which] + start * LANES
        here = held.at[:, :, span(at * LANES, size)]
        for part in range(2):
            loads.append(pltpu.make_async_copy(coeffs.at[part, :, span(source, size)], here.at[part], sems.at[0, n, part]))
            loads[-1].start()
            stores.append(pltpu.make_async_copy(here.at[part], outs[n].at[part], sems.at[1, n, part]))
        at += size
    for load, store in zip(loads, stores):
        load.wait()
        store.start()
    for store in stores:
        store.wait()


def pieces(cuts, coeffs, name):
    bands = coeffs.shape[1]
    anywhere = pl.BlockSpec(memory_space=pltpu.HBM)
    return list(
        pl.pallas_call(
            functools.partial(pieces_body, cuts),
            in_specs=[anywhere],
            out_specs=[anywhere] * len(cuts),
            out_shape=[jax.ShapeDtypeStruct((2, bands, size * LANES), BF16) for _, _, size in cuts],
            scratch_shapes=[
                pltpu.VMEM((2, bands, sum(size for _, _, size in cuts) * LANES), BF16),
                pltpu.SemaphoreType.DMA((2, len(cuts), 2)),
            ],
            compiler_params=pltpu.CompilerParams(vmem_limit_bytes=VMEM_BYTES),
            cost_estimate=pl.CostEstimate(flops=1000, bytes_accessed=1000, transcendentals=0),
            name=name,
        )(coeffs)
    )


def final_body(diag, own, far, far_1, core, up_y, across, up_z, marked, result, out, sems):
    bands = out.shape[2]
    first, side, _ = position()
    first, low = first == 1, side == 0
    wide = lambda tile: unpack(tile.astype(F32))
    mine = own[...] + wide(core[...])
    middle = wide(across[...])
    near1 = jnp.where(first, mine, wide(far_1[...]) + middle)
    near2 = wide(far[0]) + wide(up_y[0])
    away1 = jnp.where(first, middle + wide(up_z[0]), mine)
    away2 = wide(up_y[1]) + wide(up_z[1])
    above = [jnp.where(low, near1, away1), jnp.where(low, near2, away2)]
    below = [jnp.where(low, away1, near1), jnp.where(low, away2, near2)]
    copies = []
    for a in range(3):
        rows = slice(a * bands, (a + 1) * bands)
        turned = [tile[rows].T for tile in (below[1], below[0])]
        for part in range(2):
            span = slice(part * bands, (part + 1) * bands)
            mirrored = [-tile[span] if part == 0 else tile[span] for tile in turned]
            straight = [tile[rows, span] for tile in (diag, *above)]
            out[a, part] = jnp.concatenate(mirrored + straight, axis=1)
        copies.append(pltpu.make_async_copy(out.at[a], result.at[a], sems.at[a]))
        copies[-1].start()
    for copy in copies:
        copy.wait()


def final(bands, *operands):
    vmem = pl.BlockSpec(memory_space=pltpu.VMEM)
    return pl.pallas_call(
        final_body,
        in_specs=[vmem] * len(operands),
        out_specs=pl.BlockSpec(memory_space=pltpu.HBM),
        out_shape=jax.ShapeDtypeStruct((3, 2, bands, SPAN * bands), F32),
        scratch_shapes=[pltpu.VMEM((3, 2, bands, SPAN * bands), F32), pltpu.SemaphoreType.DMA((3,))],
        compiler_params=pltpu.CompilerParams(vmem_limit_bytes=VMEM_BYTES),
        name="final",
    )(*operands)


def routes(groups):
    at = lambda q, side, core: 4 * q + 2 * side + core
    away = lambda q, side: q + 1 - 2 * side
    both = [(q, side) for q in range(groups // 4) for side in (0, 1)]
    ok = [(q, s) for q, s in both if 0 <= away(q, s) < groups // 4]
    z = [(at(away(q, s), s, c), at(q, s, c)) for q, s in ok for c in (0, 1)]
    return dict(
        core=[(at(q, s, c), at(q, s, 1 - c)) for q, s in both for c in (0, 1)],
        y=[(at(q, s, c), at(q, 1 - s, c)) for q, s in both for c in (0, 1)],
        z=z,
        back=[(b, a) for a, b in z],
        across=[(at(q, s, c), at(q, 1 - s, 1 - c)) for q, s in both for c in (0, 1)],
    )


def shards(coeffs, k_plus_g, pairs, levels):
    groups = lax.axis_size("blk")
    bands, plane = coeffs.shape[1:]
    tiles = plane // 2 // LANES
    way = routes(groups)
    send = lambda value, name: lax.ppermute(value, "blk", way[name])
    tie = lambda *arrays: lax.optimization_barrier(arrays)

    begins = [sum(CHUNKS[:i]) for i in range(len(CHUNKS))]
    last = len(CHUNKS) - 1
    y_blocks, z_blocks = [[block] for block in pieces([("y", 0, CHUNKS[0]), ("z", 0, CHUNKS[0])], coeffs, "one")]
    levels, coeffs, y_blocks[0], z_blocks[0] = tie(levels, coeffs, y_blocks[0], z_blocks[0])
    swapped = send(coeffs, "core")
    facts = facts_of(levels, pairs)
    coeffs, facts = tie(coeffs, facts)
    here, facts_core = [(facts, None, 0)], send(facts, "core")
    facts_y, facts_z = send(jnp.concatenate([facts, facts_core], axis=0), "y"), send(facts, "z")
    cuts = [(which, begins[i], CHUNKS[i]) for i in range(1, last + 1) for which in ("y", "z")]
    blocks = pieces(cuts, coeffs, "rest")
    y_blocks += blocks[0::2]
    z_blocks += blocks[1::2]
    got_y, got_z = [], []
    for y_block, z_block in zip(y_blocks, z_blocks):
        got_y.append(send(y_block, "y"))
        got_z.append(send(z_block, "z"))

    coeffs, y_blocks[-1], z_blocks[-1] = tie(coeffs, y_blocks[-1], z_blocks[-1])
    (diag,) = pair_sums("diag", k_plus_g, [[(coeffs, None, 0)]], 0, 2 * tiles, [here])
    diag, swapped, coeffs = tie(diag, swapped, coeffs)
    own, own_packed = pair_sums(
        "near", k_plus_g, [[(swapped, "core", 0)], [(coeffs, "core", 0)]], 0, tiles, [[(facts_core, None, 0)], here]
    )
    tile_own = send(own_packed, "core")
    sums, before = None, own
    for i, (begin, size) in enumerate(zip(begins, CHUNKS)):
        blocks = lambda other: [[(got_y[i], None, 0)], [(coeffs, "side", begin)], [(got_z[i], None, 0)], [(other, None, 0)]]
        if i < last:
            got_y[i], got_z[i], before = tie(got_y[i], got_z[i], before)
            if i == 0:
                own = before
            else:
                sums = before
            (sums,) = pair_sums("far", k_plus_g, blocks(send(got_y[i], "core")), begin, size, start=sums)
            before = sums
        else:
            got_y[i], sums, tile_own = tie(got_y[i], sums, tile_own)
            marked = mark(got_z[i], facts_y, facts_z)
            other, marked = tie(send(got_y[i], "core"), marked)
            pairs_02, pairs_12, pair_1 = pair_sums(
                "far", k_plus_g, blocks(other), begin, size,
                [[(facts_y, None, 0)], here, [(facts_z, None, 0)], [(facts_y, None, 1)]], sums,
            )
    tile_y = send(pairs_02, "y")
    tile_across = send(pair_1, "across")
    tile_z = send(pairs_12, "back")
    return final(bands, diag, own, pairs_02, pair_1, tile_own, tile_y, tile_across, tile_z, marked)


def solution(mesh):
    in_specs = (
        P(None, ("snap", "blk"), None),
        P("snap", None),
        P(("snap", "blk"), None),
        P(("snap", "blk")),
    )
    out_specs = P(None, None, ("snap", "blk"), None)
    return jax.shard_map(shards, mesh=mesh, in_specs=in_specs, out_specs=out_specs, check_vma=False)
```
